32 devices in a mesh: dp: 8 (over y, x, core), section: 4 (over z).
Axes of the slice: x: 2, y: 2, z: 4, core: 2. Of those that a mesh axis runs over, the one named last changes fastest.
Arguments:
- images: bfloat16 [6, 32, 196, 384], P(None, 'dp'), may hold values from -6 to 6
- out_grad: bfloat16 [6, 32, 196, 384], P(None, 'dp'), may hold values from -6 to 6
- padding: int32 [6, 32], P(None, 'dp'), may hold values 0 or 1
- affine_scale: bfloat16 [4, 384], replicated, may hold values from 0.5 to 1.5
- affine_shift: bfloat16 [4, 384], replicated, may hold values from -3 to 3
- layer_scale: bfloat16 [4, 384], replicated, may hold values from 0.29882812 to 1.5
- patch_weight: bfloat16 [2, 196, 196], replicated, may hold values from -0.4375 to 0.4375
- patch_bias: bfloat16 [2, 196], replicated, may hold values from -3 to 3
- up_weight: bfloat16 [2, 384, 1536], replicated, may hold values from -0.3125 to 0.3125
- up_bias: bfloat16 [2, 1536], replicated, may hold values from -3 to 3
- down_weight: bfloat16 [2, 1536, 384], replicated, may hold values from -0.15625 to 0.15625
- down_bias: bfloat16 [2, 384], replicated, may hold values from -2 to 2
Outputs:
- section_outputs: bfloat16 [4, 6, 32, 196, 384], P('section', None, 'dp')
- section_input_grads: bfloat16 [4, 6, 32, 196, 384], P('section', None, 'dp')
- scale_grads: float32 [4, 384], replicated
- shift_grads: float32 [4, 384], replicated
- gain_grads: float32 [4, 384], replicated
- tile_projection_slopes: float32 [2, 196, 196], replicated
- offset_grads: float32 [2, 196], replicated
- upward_grads: float32 [2, 384, 1536], replicated
- upbias_grads: float32 [2, 1536], replicated
- downward_grads: float32 [2, 1536, 384], replicated
- downbias_grads: float32 [2, 384], replicated
The draws below stay inside these ranges and needn't reach their ends.
All inputs are finite; a program needn't handle non-finite values. No bound on the sum of `padding` on one device may be relied on, other than what follows from the above.
Results may differ from the reference program's by a relative error of at most 0.012.
The reference program's roundings to bfloat16 on the way count: a program that leaves them out, or rounds other values in their place, can miss the bound.
Values may be sent and summed in bfloat16 or wider, within the bound.
A program may use at most 128 MiB of HBM per device.

```python
import math
import jax
import jax.numpy as jnp
from jax import lax

D = 384
H = 1536
P_SIZE = 196
LAYERS = 2
MB = 6
IMAGES = 32
N_SECTION = 4


def with_ends(values, key, low, high):
    place = [jax.random.randint(jax.random.fold_in(key, axis), (), 0, length) for axis, length in enumerate(values.shape)]
    widest = values.shape.index(max(values.shape))
    beside = place[:widest] + [(place[widest] + 1) % values.shape[widest]] + place[widest + 1:]
    return values.at[tuple(place)].set(low).at[tuple(beside)].set(high)


def block_levels(rng, dims, pieces, smallest, top_value):
    level, own = 1.0, jax.random.fold_in(rng, 6)
    for dim, blocks in pieces:
        heights = jnp.exp(jax.random.uniform(jax.random.fold_in(own, dim), (blocks,), jnp.float32, smallest / len(pieces), top_value / len(pieces)))
        level = level * jnp.repeat(heights, dims[dim] // blocks).reshape([-1 if axis == dim else 1 for axis in range(len(dims))])
    return level


def bell_draw(stream_key, dims, spread, reach, cuts=(), kind=jnp.bfloat16):
    drawn = jax.random.normal(stream_key, dims, jnp.float32) * spread
    if len(cuts) > 0:
        drawn = block_levels(stream_key, dims, cuts, -0.22, 0.18) * drawn
    return jnp.clip(drawn, min=-reach, max=reach).astype(kind)


def setup_inputs(seed: int = 0) -> dict:
    arg_keys = jax.random.split(jax.random.key(seed), 13)
    images = bell_draw(arg_keys[0], (MB, IMAGES, P_SIZE, D), 1.0, 6.0, ((1, 8),))
    out_grad = bell_draw(arg_keys[1], (MB, IMAGES, P_SIZE, D), 1.0, 6.0, ((1, 8),))
    padding = with_ends((jax.random.randint(arg_keys[2], (MB, IMAGES), 0, 4) < 3).astype(jnp.int32), jax.random.fold_in(arg_keys[2], 1), 0, 1)
    affine_scale = jnp.clip(1.0 + 0.1 * jax.random.normal(arg_keys[3], (N_SECTION, D), jnp.float32), 0.5, 1.5).astype(jnp.bfloat16)
    affine_shift = bell_draw(arg_keys[4], (N_SECTION, D), 0.5, 3.0)
    layer_scale = jnp.clip(jnp.exp(jax.random.uniform(arg_keys[5], (N_SECTION, D), jnp.float32, math.log(0.29882812), math.log(1.5))), 0.29882812, 1.5).astype(jnp.bfloat16)
    patch_weight = bell_draw(arg_keys[6], (LAYERS, P_SIZE, P_SIZE), P_SIZE ** -0.5, 0.4375)
    patch_bias = bell_draw(arg_keys[7], (LAYERS, P_SIZE), 0.5, 3.0)
    up_weight = bell_draw(arg_keys[8], (LAYERS, D, H), D ** -0.5, 0.3125)
    up_bias = bell_draw(arg_keys[9], (LAYERS, H), 0.5, 3.0)
    down_weight = bell_draw(arg_keys[10], (LAYERS, H, D), H ** -0.5, 0.15625)
    down_bias = bell_draw(arg_keys[11], (LAYERS, D), 0.3, 2.0)
    return dict(images=images, out_grad=out_grad, padding=padding, affine_scale=affine_scale, affine_shift=affine_shift, layer_scale=layer_scale, patch_weight=patch_weight, patch_bias=patch_bias, up_weight=up_weight, up_bias=up_bias, down_weight=down_weight, down_bias=down_bias)


@jax.custom_vjp
def low(v):
    return lax.optimization_barrier(v.astype(jnp.bfloat16)).astype(jnp.float32)

@jax.custom_vjp
def low_back(v):
    return v

def low_keep(v):
    return (low(v), None)

def low_pass(kept, grad):
    return (grad,)

def back_keep(v):
    return (v, None)

def back_low(kept, grad):
    return (low(grad),)
low.defvjp(low_keep, low_pass)
low_back.defvjp(back_keep, back_low)

def patch_half(xin, alpha, beta, gain, weight_matrix, bias_vector):
    normalized_input = low(alpha * xin + beta)
    mixing_output = jnp.einsum('nk,gkw->gnw', weight_matrix, normalized_input, precision=lax.Precision.HIGHEST) + bias_vector[None, :, None]
    mixing_output = low_back(mixing_output)
    return low(xin + gain * mixing_output)

def channel_half(xin, alpha, beta, gain, w_up, b_up, w_down, b_down):
    normalized_input = low(alpha * xin + beta)
    pre = low_back(jnp.einsum('bpd,dh->bph', normalized_input, w_up, precision=lax.Precision.HIGHEST) + b_up)
    hidden = low(jax.nn.gelu(pre))
    residual_path = low_back(jnp.einsum('bph,hd->bpd', hidden, w_down, precision=lax.Precision.HIGHEST) + b_down)
    return low(xin + gain * residual_path)

def chain(params, start, offsets):
    a_scale, a_shift, gains, p_weight, p_bias, u_weight, u_bias, d_weight, d_bias = params
    outputs = []
    current = start
    for half in range(N_SECTION):
        xin = low_back(current + offsets[half])
        layer = half // 2
        if half % 2 == 0:
            current = patch_half(xin, a_scale[half], a_shift[half], gains[half], p_weight[layer], p_bias[layer])
        else:
            current = channel_half(xin, a_scale[half], a_shift[half], gains[half], u_weight[layer], u_bias[layer], d_weight[layer], d_bias[layer])
        outputs.append(current)
    return jnp.stack(outputs)

def reference(images, out_grad, padding, affine_scale, affine_shift, layer_scale, patch_weight, patch_bias, up_weight, up_bias, down_weight, down_bias):
    params = tuple((a.astype(jnp.float32) for a in (affine_scale, affine_shift, layer_scale, patch_weight, patch_bias, up_weight, up_bias, down_weight, down_bias)))
    live = padding.astype(jnp.float32)[:, :, None, None]
    starts = images.astype(jnp.float32) * live
    cotangents = out_grad.astype(jnp.float32) * live

    def one_batch(carry, pair):
        start, cotangent = pair
        offsets = jnp.zeros((N_SECTION,) + start.shape, jnp.float32)
        outputs, pull = jax.vjp(chain, params, start, offsets)
        full = jnp.zeros_like(outputs).at[N_SECTION - 1].set(cotangent)
        grad_params, grad_start, grad_offsets = pull(full)
        carry = jax.tree.map(lambda left, right: left + right, carry, grad_params)
        return (carry, (outputs.astype(jnp.bfloat16), grad_offsets.astype(jnp.bfloat16)))
    init = tuple((jnp.zeros_like(p) for p in params))
    totals, (outputs, in_grads) = lax.scan(one_batch, init, (starts, cotangents))
    outputs = jnp.transpose(outputs, (1, 0, 2, 3, 4))
    in_grads = jnp.transpose(in_grads, (1, 0, 2, 3, 4))
    return (outputs, in_grads, totals[0], totals[1], totals[2], totals[3], totals[4], totals[5], totals[6], totals[7], totals[8])
```

```python
import functools

import jax
import jax.numpy as jnp
from jax import lax
from jax.experimental import pallas as pl
from jax.experimental.pallas import tpu as pltpu
from jax.sharding import PartitionSpec as P

f32, bf16 = jnp.float32, jnp.bfloat16
C0 = 0.7978845608028654
C1 = 0.044715
SMALL_ROWS = 12
ROW_SCALE, ROW_SHIFT, ROW_GAIN, ROW_OFFSET, ROW_UPB = 0, 2, 4, 6, 7


def dot(a, b, ca=1, cb=0):
    return lax.dot_general(a, b, (((ca,), (cb,)), ((), ())), preferred_element_type=f32)


def up_to(n, k):
    return -(-n // k) * k


def gelu_parts(pre):
    pre = pre.astype(bf16)
    c0, c01, c03 = bf16(C0), bf16(C0 * C1), bf16(3 * C0 * C1)
    half, one = bf16(0.5), bf16(1.0)
    square = pre * pre
    t = jnp.tanh(pre * (c0 + c01 * square))
    hx = half * pre
    return hx + hx * t, (half + half * t) + hx * (one - t * t) * (c0 + c03 * square)


def plan(sec, t, M):
    half = M // 2
    mine = t < half
    m = lax.rem(t + half * lax.rem(sec, 2), M)
    yes = sec >= 0
    return dict(
        m=m, mine=mine, ffn0=yes, patch1=yes, up1=yes, down1=sec == 3,
        back_ffn1=yes, back_patch1=(sec < 3) | mine, back_ffn0=sec < 2, back_patch0=(sec == 0) | ((sec == 1) & mine),
    )


def compute_kernel(NC, RC, get_sec, live_ref, img_h, og_h, ac, sh, ls, pw_in, pb_in, wu_h, bu, wd_h, bd, out_h, gin_h, grad_o,
                   img, og, outs, gins, wu, wd, pw, rs, kk, aa, bdl, wus, wds, bus, stage, xw, xt, gw, gt, hid, slope, dpre,
                   gx, gd, gp, gsum, sd, bup, gdn, in_sem, out_sem, w_sem):
    M, P, B, D = img.shape
    L, _, H = wu.shape
    PP = pw.shape[1]
    R = B * PP
    sec = get_sec()
    own = sec // 2

    def rows(b):
        return slice(b * PP, (b + 1) * PP)

    def cols(b):
        return slice(b * D, (b + 1) * D)

    def vec(ref, k):
        return ref[k:k + 1, :].astype(f32)

    def load(t, which):
        m = plan(sec, t, M)["m"]
        return pltpu.make_async_copy((img_h, og_h)[which].at[m], (img, og)[which].at[m], in_sem.at[which, m])

    load(0, 0).start()
    w_up = pltpu.make_async_copy(wu_h, wu, w_sem.at[0])
    w_down = pltpu.make_async_copy(wd_h, wd, w_sem.at[1])
    w_up.start()
    w_down.start()
    load(0, 1).start()
    for t in range(1, M):
        load(t, 0).start()
        load(t, 1).start()

    pw[...] = jnp.zeros_like(pw)
    pbt = jnp.concatenate([pb_in[...].astype(f32), jnp.zeros((8 - L, P), f32)], axis=0).T
    stage[...] = jnp.zeros_like(stage)
    for l in range(L):
        pw[l, :P, :P] = pw_in[:, l, :]
        rs[l] = jnp.sum(pw[l].astype(f32), axis=1, keepdims=True)
        stage[0:P, l:l + 1] = pbt[:, l:l + 1]
        kk[l] = vec(ls, 2 * l) * (vec(sh, 2 * l) * rs[l] + stage[0:PP, l:l + 1])
        aa[l] = vec(ac, 2 * l) * vec(ls, 2 * l)
        bdl[l] = vec(bd, l) * vec(ls, 2 * l + 1)
    stage[0:PP, 0:128] = jnp.zeros((PP, 128), f32)
    for r in (gx, gd, gp, gsum, sd, bup, gdn):
        r[...] = jnp.zeros_like(r)
    w_up.wait()
    w_down.wait()
    for l in range(L):
        acol = jnp.broadcast_to(vec(ac, 2 * l + 1), (8, D)).T[:, 0:1]
        shift8 = jnp.broadcast_to(vec(sh, 2 * l + 1), (8, D)).astype(bf16)
        for k in range(0, H, D):
            wus[l, :, k:k + D] = (wu[l, :, k:k + D].astype(f32) * acol).astype(bf16)
            wds[l, k:k + D, :] = (wd[l, k:k + D, :].astype(f32) * vec(ls, 2 * l + 1)).astype(bf16)
            bus[l, :, k:k + D] = dot(shift8, wu[l, :, k:k + D])[0:1, :] + bu[l:l + 1, k:k + D].astype(f32)

    def take(ref, m):
        v = jnp.swapaxes(ref[m].astype(f32), 0, 1)
        for b in range(B):
            stage[b * PP:b * PP + P, :] = v[b] * live_ref[b, m].astype(f32)
            stage[b * PP + P:(b + 1) * PP, :] = jnp.zeros((PP - P, D), f32)

    def give(which, m, pieces):
        v = jnp.stack([p[0:P, :] for p in pieces], axis=0)
        (outs, gins)[which][m] = jnp.swapaxes(v, 0, 1).astype(bf16)
        pltpu.make_async_copy((outs, gins)[which].at[m], (out_h, gin_h)[which].at[m], out_sem.at[which, m]).start()

    def chunk(c):
        return pl.ds(pl.multiple_of(c * NC, NC), NC)

    def row_chunk(r):
        return pl.ds(pl.multiple_of(r * RC, RC), RC)

    def step(t, carry):
        p = plan(sec, t, M)
        m = p["m"]
        load(t, 0).wait()
        take(img, m)
        for b in range(B):
            xw[0, :, cols(b)] = stage[rows(b), :].astype(bf16)

        def forward(l, carry):
            @pl.when((l == 0) | p["patch1"])
            def _():
                mix = dot(pw[l], xw[l])
                new = [xw[l, :, cols(b)].astype(f32) + (aa[l] * mix[:, cols(b)] + kk[l]) for b in range(B)]
                xt[l] = jnp.concatenate(new, axis=0).astype(bf16)

                @pl.when(sec == 2 * l)
                def _():
                    give(0, m, new)

            @pl.when(jnp.where(l == 0, p["ffn0"], p["up1"]))
            def _():
                def up(c, carry):
                    pre = dot(xt[l], wus[l, :, chunk(c)]) + bus[l, :, chunk(c)]
                    h, s = gelu_parts(pre)
                    hid[l, :, chunk(c)] = h
                    slope[l, :, chunk(c)] = s
                    return carry
                lax.fori_loop(0, H // NC, up, 0)

            @pl.when(jnp.where(l == 0, p["ffn0"], p["down1"]))
            def _():
                def down(r, carry):
                    q = row_chunk(r)
                    stage[q, :] = xt[l, q, :].astype(f32) + (dot(hid[l, q, :], wds[l]) + bdl[l])
                    return carry
                lax.fori_loop(0, R // RC, down, 0)

                @pl.when(l + 1 < L)
                def _():
                    for b in range(B):
                        xw[l + 1, :, cols(b)] = stage[rows(b), :].astype(bf16)

                @pl.when(sec == 2 * l + 1)
                def _():
                    give(0, m, [stage[rows(b), :] for b in range(B)])
            return carry

        lax.fori_loop(0, L, forward, 0)

        load(t, 1).wait()

        @pl.when(p["back_ffn1"])
        def _():
            take(og, m)
            gt[...] = stage[...].astype(bf16)

        def backward(i, carry):
            l = L - 1 - i
            weights = p["mine"] & (own == l)

            @pl.when(jnp.where(l == 0, p["back_ffn0"], p["back_ffn1"]))
            def _():
                def dh(c, carry):
                    d = dot(gt[...], wds[l, chunk(c), :], 1, 1)
                    dpre[:, chunk(c)] = (d * slope[l, :, chunk(c)].astype(f32)).astype(bf16)
                    return carry
                lax.fori_loop(0, H // NC, dh, 0)

                def du(r, carry):
                    q = row_chunk(r)
                    stage[q, :] = gt[q, :].astype(f32) + dot(dpre[q, :], wus[l], 1, 1)
                    return carry
                lax.fori_loop(0, R // RC, du, 0)

                @pl.when(weights)
                def _():
                    gdn[...] += jnp.sum(gt[...].astype(f32), axis=0, keepdims=True)
                    g_t = gt[...].T
                    x_t = xt[l].T

                    def grads(c, carry):
                        q = chunk(c)
                        d = dpre[:, q]
                        gx[:, q] += dot(x_t, d)
                        gd[:, q] += dot(g_t, hid[l, :, q])
                        bup[:, q] += jnp.sum(d.astype(f32), axis=0, keepdims=True)
                        return carry
                    lax.fori_loop(0, H // NC, grads, 0)
                for b in range(B):
                    gw[:, cols(b)] = stage[rows(b), :].astype(bf16)

                @pl.when(sec == 2 * l + 1)
                def _():
                    give(1, m, [stage[rows(b), :] for b in range(B)])

            @pl.when(jnp.where(l == 0, p["back_patch0"], p["back_patch1"]))
            def _():
                back = dot(pw[l], gw[...], 0, 0)
                new = [gw[:, cols(b)].astype(f32) + aa[l] * back[:, cols(b)] for b in range(B)]
                gt[...] = jnp.concatenate(new, axis=0).astype(bf16)

                @pl.when(sec == 2 * l)
                def _():
                    give(1, m, new)

                @pl.when(weights)
                def _():
                    scaled = jnp.concatenate([(gw[:, cols(b)].astype(f32) * aa[l]).astype(bf16) for b in range(B)], axis=1)
                    gp[...] += dot(scaled, xw[l], 1, 1)
                    for b in range(B):
                        gsum[...] += gw[:, cols(b)].astype(f32)
                        sd[...] += jnp.sum(back[:, cols(b)] * xw[l, :, cols(b)].astype(f32), axis=0, keepdims=True)
            return carry

        lax.fori_loop(0, L, backward, 0)
        return carry

    lax.fori_loop(0, M, step, 0)

    for l in range(L):
        @pl.when(own == l)
        def _():
            acol = jnp.broadcast_to(vec(ac, 2 * l + 1), (8, D)).T[:, 0:1]
            ccol = jnp.broadcast_to(vec(sh, 2 * l + 1), (8, D)).T[:, 0:1]
            scale1 = jnp.zeros((D, 1), f32)
            shift1 = jnp.zeros((D, 1), f32)
            for k in range(0, H, D):
                g = gx[:, k:k + D]
                w = wu[l, :, k:k + D].astype(f32)
                b = bup[:, k:k + D]
                grad_o[k:k + D, :] = (acol * g + ccol * b).astype(bf16)
                scale1 += jnp.sum(w * g, axis=1, keepdims=True)
                shift1 += jnp.sum(w * b, axis=1, keepdims=True)
            gain1 = vec(bd, l) * gdn[...]
            for k in range(0, H, D):
                g = gd[:, k:k + D].T
                gain1 += jnp.sum(g * wd[l, k:k + D, :].astype(f32), axis=0, keepdims=True)
                grad_o[H + k:H + k + D, :] = (g * vec(ls, 2 * l + 1)).astype(bf16)
            both = jnp.broadcast_to(jnp.concatenate([scale1, shift1], axis=1), (D, 2)).T
            gs = gsum[...]
            lsrow, crow = vec(ls, 2 * l), vec(sh, 2 * l)
            wsum = jnp.sum(gs * rs[l], axis=0, keepdims=True)
            stage[0:PP, 0:PP] = gp[...] + jnp.sum(gs * (lsrow * crow), axis=1, keepdims=True)
            stage[0:PP, 256:257] = jnp.zeros((PP, 1), f32)
            stage[0:P, 256:257] = pbt[:, l:l + 1]
            psum = jnp.sum(gs * stage[0:PP, 256:257], axis=0, keepdims=True)
            offset = jnp.broadcast_to(jnp.sum(gs * lsrow, axis=1, keepdims=True), (PP, 8)).T[0:1, :]
            s_row = sd[...]
            extra = P + SMALL_ROWS

            def put(k, row):
                stage[P + k:P + k + 1, 0:row.shape[1]] = row
            stage[P:extra, :] = jnp.zeros((SMALL_ROWS, D), f32)
            put(ROW_SCALE, lsrow * s_row)
            put(ROW_SCALE + 1, both[0:1, :])
            put(ROW_SHIFT, lsrow * wsum)
            put(ROW_SHIFT + 1, both[1:2, :])
            put(ROW_GAIN, vec(ac, 2 * l) * s_row + crow * wsum + psum)
            put(ROW_GAIN + 1, gain1)
            put(ROW_OFFSET, offset[:, 0:P])
            for k in range(H // D):
                put(ROW_UPB + k, bup[:, k * D:(k + 1) * D])
            put(ROW_UPB + H // D, vec(ls, 2 * l + 1) * gdn[...])
            grad_o[2 * H:2 * H + extra, :] = stage[0:extra, :].astype(bf16)
    grad_o[2 * H + P + SMALL_ROWS:, :] = jnp.zeros((grad_o.shape[0] - 2 * H - P - SMALL_ROWS, D), bf16)
    for m in range(M):
        for which in range(2):
            pltpu.make_async_copy((outs, gins)[which].at[m], (out_h, gin_h)[which].at[m], out_sem.at[which, m]).wait()


def compute_call(get_sec, grad_rows, images, out_grad, live, ac, sh, ls, pw, pb, wu, bu, wd, bd, NC=1536, RC=800):
    M, P, B, D = images.shape
    L, _, H = wu.shape
    PP = up_to(P, 8)
    R = B * PP
    vm = pl.BlockSpec(memory_space=pltpu.VMEM)
    hbm = pl.BlockSpec(memory_space=pl.ANY)
    return pl.pallas_call(
        functools.partial(compute_kernel, NC, RC, get_sec),
        in_specs=[pl.BlockSpec(memory_space=pltpu.SMEM), hbm, hbm, vm, vm, vm, vm, vm, hbm, vm, hbm, vm],
        out_specs=[hbm, hbm, vm],
        out_shape=[jax.ShapeDtypeStruct(images.shape, bf16)] * 2 + [jax.ShapeDtypeStruct((grad_rows, D), bf16)],
        scratch_shapes=[
            pltpu.VMEM(images.shape, bf16), pltpu.VMEM(images.shape, bf16), pltpu.VMEM(images.shape, bf16), pltpu.VMEM(images.shape, bf16),
            pltpu.VMEM((L, D, H), bf16), pltpu.VMEM((L, H, D), bf16),
            pltpu.VMEM((L, PP, PP), bf16), pltpu.VMEM((L, PP, 1), f32), pltpu.VMEM((L, PP, D), f32), pltpu.VMEM((L, 1, D), f32), pltpu.VMEM((L, 1, D), f32),
            pltpu.VMEM((L, D, H), bf16), pltpu.VMEM((L, H, D), bf16), pltpu.VMEM((L, 1, H), f32),
            pltpu.VMEM((R, D), f32),
            pltpu.VMEM((L, PP, B * D), bf16), pltpu.VMEM((L, R, D), bf16), pltpu.VMEM((PP, B * D), bf16), pltpu.VMEM((R, D), bf16),
            pltpu.VMEM((L, R, H), bf16), pltpu.VMEM((L, R, H), bf16), pltpu.VMEM((R, H), bf16),
            pltpu.VMEM((D, H), f32), pltpu.VMEM((D, H), f32), pltpu.VMEM((PP, PP), f32), pltpu.VMEM((PP, D), f32),
            pltpu.VMEM((1, D), f32), pltpu.VMEM((1, H), f32), pltpu.VMEM((1, D), f32),
            pltpu.SemaphoreType.DMA((2, M)), pltpu.SemaphoreType.DMA((2, M)), pltpu.SemaphoreType.DMA((2,)),
        ],
        compiler_params=pltpu.CompilerParams(vmem_limit_bytes=60 * 2**20),
        name="chain",
    )(live, images, out_grad, ac, sh, ls, pw, pb, wu, bu, wd, bd)


def bits_of(n):
    return n.bit_length() - 1


def reduce_unit(n_dp):
    return 16 * n_dp


def reduce_kernel(n_dp, n_sec, g_ref, full, work, recv, send_sem, recv_sem, z_send, z_recv, g_send, g_recv):
    nb = bits_of(n_dp)
    half = full.shape[1] // 2
    unit = reduce_unit(n_dp)
    part_a = up_half = -(-(half // unit) // 2) * unit
    parts = [(0, part_a), (part_a, half - part_a)]
    parts = [p for p in parts if p[1] > 0]
    me = lax.axis_index("dp")
    sec = lax.axis_index("section")
    layer = sec // 2
    rest = list(range(1, nb))
    orders = [rest, rest[::-1]]
    bit = [(me // (1 << j)) % 2 for j in range(nb)]
    zbit = sec % 2

    def peer(j):
        return (me + (1 << j) - 2 * (1 << j) * bit[j], sec)

    zpeer = (me, sec + 1 - 2 * zbit)

    barrier = pltpu.get_barrier_semaphore()
    for j in range(nb):
        pl.semaphore_signal(barrier, inc=1, device_id=peer(j), device_id_type=pl.DeviceIdType.MESH)

    @pl.when(sec > 0)
    def _():
        pl.semaphore_signal(barrier, inc=1, device_id=(me, sec - 1), device_id_type=pl.DeviceIdType.MESH)

    @pl.when(sec < n_sec - 1)
    def _():
        pl.semaphore_signal(barrier, inc=1, device_id=(me, sec + 1), device_id_type=pl.DeviceIdType.MESH)

    pl.semaphore_wait(barrier, nb + jnp.where(sec > 0, 1, 0) + jnp.where(sec < n_sec - 1, 1, 0))

    def copy(src, dst, s, r, device):
        return pltpu.make_async_remote_copy(src_ref=src, dst_ref=dst, send_sem=s, recv_sem=r, device_id=device, device_id_type=pl.DeviceIdType.MESH)

    def rows(off, n):
        return pl.ds(pl.multiple_of(off, 16), n)

    base = bit[0] * half
    first = copy(g_ref.at[rows((1 - bit[0]) * half, half)], recv.at[pl.ds(0, half)], send_sem.at[0, 0], recv_sem.at[0, 0], peer(0))
    first.start()
    first.wait()
    work[...] = (g_ref[rows(base, half), :].astype(f32) + recv[0:half, :].astype(f32)).astype(bf16)

    place = [jnp.int32(off) for off, _ in parts]
    size = [n for _, n in parts]
    slot = half
    for t in range(nb):
        pending = []
        for k in range(len(parts)):
            n = size[k] // 2
            if t < nb - 1:
                b, device = bit[orders[k][t]], peer(orders[k][t])
            else:
                b, device = zbit, zpeer
            c = copy(work.at[rows(place[k] + (1 - b) * n, n)], recv.at[pl.ds(slot, n)], send_sem.at[k, t + 1], recv_sem.at[k, t + 1], device)
            c.start()
            pending.append((c, place[k] + b * n, n, slot))
            slot += n
        for k, (c, keep, n, at) in enumerate(pending):
            c.wait()
            total = work[rows(keep, n), :].astype(f32) + recv[at:at + n, :].astype(f32)
            if t < nb - 1:
                work[rows(keep, n), :] = total.astype(bf16)
            else:
                full[layer, rows(base + keep, n), :] = total.astype(bf16)
            place[k], size[k] = keep, n

    def piece(k, j):
        return full.at[j // 2, rows(base + place[k] + (j % 2 - zbit) * size[k], size[k])]

    def z_copies(k, j, d):
        target = sec + (1 if d == 0 else -1)
        return copy(piece(k, j), piece(k, j), z_send.at[k, d, abs_step(j)], z_recv.at[k, d, abs_step(j, 1)], (me, target))

    def abs_step(j, more=0):
        return more + jnp.where(j > sec, j - sec, sec - j)

    def z_send_item(dist, d):
        j = sec - dist if d == 0 else sec + dist
        target = sec + 1 if d == 0 else sec - 1
        ok = (j >= 0) & (target < n_sec) if d == 0 else (j < n_sec) & (target >= 0)

        @pl.when(ok)
        def _():
            for k in range(len(parts)):
                copy(piece(k, j), piece(k, j), z_send.at[k, d, dist], z_recv.at[k, d, dist], (me, target)).start()

    def z_wait_send(dist, d):
        j = sec - dist if d == 0 else sec + dist
        target = sec + 1 if d == 0 else sec - 1
        ok = (j >= 0) & (target < n_sec) if d == 0 else (j < n_sec) & (target >= 0)

        @pl.when(ok)
        def _():
            for k in range(len(parts)):
                copy(piece(k, j), piece(k, j), z_send.at[k, d, dist], z_recv.at[k, d, dist], (me, target)).wait_send()

    def z_wait_recv(dist, d):
        j = sec - dist - 1 if d == 0 else sec + dist + 1
        target = sec + 1 if d == 0 else sec - 1
        ok = (j >= 0) if d == 0 else (j < n_sec)

        @pl.when(ok)
        def _():
            for k in range(len(parts)):
                copy(piece(k, j), piece(k, j), z_send.at[k, d, dist], z_recv.at[k, d, dist], (me, sec)).wait_recv()

    def region(k, t):
        order = orders[k]
        off, n = jnp.int32(parts[k][0]), parts[k][1]
        for j in order[:len(order) - t]:
            n = n // 2
            off = off + bit[j] * n
        return off, n

    def g_copy(which, k, t, l):
        off, n = region(k, t)
        j = orders[k][len(orders[k]) - 1 - t]
        ref = full.at[l, rows(base + off, n)]
        return copy(ref, ref, g_send.at[which, k, t], g_recv.at[which, k, t], peer(j))

    def c_copy(which, l):
        ref = full.at[l, rows(base, half)]
        return copy(ref, ref, g_send.at[which, 0, nb - 1], g_recv.at[which, 0, nb - 1], peer(0))

    n_layer = n_sec // 2
    layers = [layer] + [(layer + i) % n_layer for i in range(1, n_layer)]
    steps = nb - 1
    for d in range(2):
        z_send_item(0, d)
    for d in range(2):
        z_wait_recv(0, d)
    for d in range(2):
        z_send_item(1, d)
    for k in range(len(parts)):
        g_copy(0, k, 0, layers[0]).start()
    for dist in range(1, n_sec - 1):
        for d in range(2):
            z_wait_recv(dist, d)
        if dist < n_sec - 2:
            for d in range(2):
                z_send_item(dist + 1, d)
        if dist <= steps:
            for k in range(len(parts)):
                g_copy(0, k, dist - 1, layers[0]).wait_recv()
                if dist < steps:
                    g_copy(0, k, dist, layers[0]).start()
    done = min(n_sec - 2, steps)
    for t in range(done, steps):
        for k in range(len(parts)):
            g_copy(0, k, t, layers[0]).wait_recv()
            if t + 1 < steps:
                g_copy(0, k, t + 1, layers[0]).start()
    c_copy(0, layers[0]).start()
    for w in range(1, n_layer):
        for t in range(steps):
            for k in range(len(parts)):
                g_copy(w, k, t, layers[w]).start()
            for k in range(len(parts)):
                g_copy(w, k, t, layers[w]).wait_recv()
        c_copy(w, layers[w]).start()
    for w in range(n_layer):
        c_copy(w, layers[w]).wait_recv()
    for w in range(n_layer):
        for t in range(steps):
            for k in range(len(parts)):
                g_copy(w, k, t, layers[w]).wait_send()
        c_copy(w, layers[w]).wait_send()
    for dist in range(n_sec - 1):
        for d in range(2):
            z_wait_send(dist, d)


def reduce_call(n_dp, n_sec, grads):
    rows, width = grads.shape
    nb = bits_of(n_dp)
    vm = pl.BlockSpec(memory_space=pltpu.VMEM)
    return pl.pallas_call(
        functools.partial(reduce_kernel, n_dp, n_sec),
        in_specs=[vm],
        out_specs=vm,
        out_shape=jax.ShapeDtypeStruct((n_sec // 2, rows, width), bf16),
        scratch_shapes=[
            pltpu.VMEM((rows // 2, width), bf16), pltpu.VMEM((rows, width), bf16),
            pltpu.SemaphoreType.DMA((2, nb + 1)), pltpu.SemaphoreType.DMA((2, nb + 1)),
            pltpu.SemaphoreType.DMA((2, 2, n_sec)), pltpu.SemaphoreType.DMA((2, 2, n_sec)),
            pltpu.SemaphoreType.DMA((n_sec // 2, 2, nb)), pltpu.SemaphoreType.DMA((n_sec // 2, 2, nb)),
        ],
        compiler_params=pltpu.CompilerParams(collective_id=1, has_side_effects=True, vmem_limit_bytes=48 * 2**20),
        name="reduce",
    )(grads)


def finish_kernel(P, full, scale_o, shift_o, gain_o, pw_o, off_o, up_o, upb_o, down_o, dnb_o):
    L = pw_o.shape[1]
    D, H = up_o.shape[1:]
    step = pl.program_id(0)
    for k in range(0, H, D):
        up_o[0, :, k:k + D] = full[0, k:k + D, :].astype(f32)
    down_o[0] = full[0, H:2 * H, :].astype(f32)
    tail = full[0, 2 * H:2 * H + up_to(P + SMALL_ROWS, 16), :].astype(f32)
    small = tail[P:P + SMALL_ROWS, :]
    for l in range(L):
        @pl.when(step == l)
        def _():
            pw_o[:, l, :] = tail[0:P, 0:P]
            for out, row in ((scale_o, ROW_SCALE), (shift_o, ROW_SHIFT), (gain_o, ROW_GAIN)):
                out[2 * l:2 * l + 2, :] = small[row:row + 2, :]
            off_o[l:l + 1, :] = small[ROW_OFFSET:ROW_OFFSET + 1, 0:P]
            for k in range(H // D):
                upb_o[l:l + 1, k * D:(k + 1) * D] = small[ROW_UPB + k:ROW_UPB + k + 1, :]
            dnb_o[l:l + 1, :] = small[ROW_UPB + H // D:ROW_UPB + H // D + 1, :]


def finish_call(full, P, H):
    L, rows, D = full.shape
    const = lambda *shape: pl.BlockSpec(shape, lambda i: (0,) * len(shape))
    return pl.pallas_call(
        functools.partial(finish_kernel, P),
        grid=(L,),
        in_specs=[pl.BlockSpec((1, rows, D), lambda i: (i, 0, 0))],
        out_specs=[const(2 * L, D), const(2 * L, D), const(2 * L, D), const(P, L, P), const(L, P),
                   pl.BlockSpec((1, D, H), lambda i: (i, 0, 0)), const(L, H), pl.BlockSpec((1, H, D), lambda i: (i, 0, 0)), const(L, D)],
        out_shape=[jax.ShapeDtypeStruct(s, f32) for s in ((2 * L, D), (2 * L, D), (2 * L, D), (P, L, P), (L, P), (L, D, H), (L, H), (L, H, D), (L, D))],
        compiler_params=pltpu.CompilerParams(vmem_limit_bytes=40 * 2**20),
        name="finish",
    )(full)


def shards(n_dp, n_sec, images, out_grad, padding, affine_scale, affine_shift, layer_scale, patch_weight, patch_bias, up_weight, up_bias, down_weight, down_bias):
    n_patch, width = images.shape[2:]
    hidden = up_weight.shape[2]
    grad_rows = up_to(2 * hidden + n_patch + SMALL_ROWS, 2 * reduce_unit(n_dp))
    outputs, in_grads, grads = compute_call(
        lambda: lax.axis_index("section"), grad_rows,
        images.transpose(0, 2, 1, 3), out_grad.transpose(0, 2, 1, 3), padding.T,
        affine_scale, affine_shift, layer_scale, patch_weight.transpose(1, 0, 2), patch_bias,
        up_weight, up_bias, down_weight, down_bias,
    )
    full = reduce_call(n_dp, n_sec, grads)
    scale, shift, gain, slopes, offset, up, upb, down, dnb = finish_call(full, n_patch, hidden)
    native = lambda a: a.transpose(0, 2, 1, 3)[None]
    return native(outputs), native(in_grads), scale, shift, gain, slopes.transpose(1, 0, 2), offset, up, upb, down, dnb


def solution(mesh):
    split = P(None, "dp", None, None)
    return jax.shard_map(
        functools.partial(shards, mesh.shape["dp"], mesh.shape["section"]),
        mesh=mesh,
        in_specs=(split, split, P(None, "dp")) + (P(),) * 9,
        out_specs=(P("section", None, "dp", None, None),) * 2 + (P(),) * 9,
        check_vma=False,
    )
```

```python
import functools

import jax
import jax.numpy as jnp
from jax import lax
from jax.experimental import pallas as pl
from jax.experimental.pallas import tpu as pltpu
from jax.sharding import PartitionSpec as P

f32, bf16 = jnp.float32, jnp.bfloat16
C0 = 0.7978845608028654
C1 = 0.044715
SMALL_ROWS = 12
ROW_SCALE, ROW_SHIFT, ROW_GAIN, ROW_OFFSET, ROW_UPB = 0, 2, 4, 6, 7


def dot(a, b, ca=1, cb=0):
    return lax.dot_general(a, b, (((ca,), (cb,)), ((), ())), preferred_element_type=f32)


def up_to(n, k):
    return -(-n // k) * k


def gelu_parts(pre):
    pre = pre.astype(bf16)
    c0, c01, c03 = bf16(C0), bf16(C0 * C1), bf16(3 * C0 * C1)
    half, one = bf16(0.5), bf16(1.0)
    square = pre * pre
    t = jnp.tanh(pre * (c0 + c01 * square))
    hx = half * pre
    return hx + hx * t, (half + half * t) + hx * (one - t * t) * (c0 + c03 * square)


def compute_kernel(live_ref, img_h, og_h, ac, sh, ls, pw_in, pb_in, wu_h, bu, wd_h, bd, out_h, gin_h, grad_o,
                   img, og, outs, gins, xch, pw, rs, kk, aa, bdl, wus, wds, bus, stage, xw, xt, gw, gt, hid, slope, dpre,
                   gx, gd, gp, gsum, sd, bup, gdn, in_sem, out_sem, w_sem, send_sem, recv_sem):
    M, P, B, D = img.shape
    L, _, H = wus.shape
    PP = pw.shape[1]
    R = B * PP
    me, sec = lax.axis_index("dp"), lax.axis_index("section")
    own, odd = sec // 2, sec % 2
    low = sec < 2
    partner = (me, sec + 1 - 2 * odd)
    half = M // 2

    def rows(b):
        return slice(b * PP, (b + 1) * PP)

    def cols(b):
        return slice(b * D, (b + 1) * D)

    def vec(ref, k):
        return ref[k:k + 1, :].astype(f32)

    def micro(t):
        return lax.rem(t + half * odd, M)

    def load(t, which):
        m = micro(t)
        return pltpu.make_async_copy((img_h, og_h)[which].at[m], (img, og)[which].at[m], in_sem.at[which, m])

    def save(which, m):
        return pltpu.make_async_copy((outs, gins)[which].at[m], (out_h, gin_h)[which].at[m], out_sem.at[which, m])

    def remote(src, dst, t):
        return pltpu.make_async_remote_copy(src_ref=src, dst_ref=dst, send_sem=send_sem.at[t], recv_sem=recv_sem.at[t], device_id=partner, device_id_type=pl.DeviceIdType.MESH)

    barrier = pltpu.get_barrier_semaphore()
    pl.semaphore_signal(barrier, inc=1, device_id=partner, device_id_type=pl.DeviceIdType.MESH)
    load(0, 0).start()
    w_up = pltpu.make_async_copy(wu_h, wus, w_sem.at[0])
    w_down = pltpu.make_async_copy(wd_h, wds, w_sem.at[1])
    w_up.start()
    w_down.start()
    load(0, 1).start()
    for t in range(1, M):
        load(t, 0).start()
        load(t, 1).start()

    pw[...] = jnp.zeros_like(pw)
    pbt = jnp.concatenate([pb_in[...].astype(f32), jnp.zeros((8 - L, P), f32)], axis=0).T
    stage[...] = jnp.zeros_like(stage)
    for l in range(L):
        pw[l, :P, :P] = pw_in[:, l, :]
        rs[l] = jnp.sum(pw[l].astype(f32), axis=1, keepdims=True)
        stage[0:P, l:l + 1] = pbt[:, l:l + 1]
        kk[l] = vec(ls, 2 * l) * (vec(sh, 2 * l) * rs[l] + stage[0:PP, l:l + 1])
        aa[l] = vec(ac, 2 * l) * vec(ls, 2 * l)
        bdl[l] = vec(bd, l) * vec(ls, 2 * l + 1)
    stage[0:PP, 0:128] = jnp.zeros((PP, 128), f32)
    for r in (gx, gd, gp, gsum, sd, bup, gdn):
        r[...] = jnp.zeros_like(r)
    w_up.wait()
    w_down.wait()
    for l in range(L):
        acol = jnp.broadcast_to(vec(ac, 2 * l + 1), (8, D)).T[:, 0:1]
        shift8 = jnp.broadcast_to(vec(sh, 2 * l + 1), (8, D)).astype(bf16)
        for k in range(0, H, D):
            bus[l, :, k:k + D] = dot(shift8, wus[l, :, k:k + D])[0:1, :] + bu[l:l + 1, k:k + D].astype(f32)
            wus[l, :, k:k + D] = (wus[l, :, k:k + D].astype(f32) * acol).astype(bf16)
            wds[l, k:k + D, :] = (wds[l, k:k + D, :].astype(f32) * vec(ls, 2 * l + 1)).astype(bf16)
    pl.semaphore_wait(barrier, 1)

    def take(ref, m):
        v = jnp.swapaxes(ref[m].astype(f32), 0, 1)
        for b in range(B):
            stage[b * PP:b * PP + P, :] = v[b] * live_ref[b, m].astype(f32)
            stage[b * PP + P:(b + 1) * PP, :] = jnp.zeros((PP - P, D), f32)

    def turned(pieces):
        return jnp.swapaxes(jnp.stack([p[0:P, :] for p in pieces], axis=0), 0, 1).astype(bf16)

    def from_tall(value):
        value = value.astype(f32)
        return turned([value[rows(b), :] for b in range(B)])

    def from_wide(value):
        return turned([value[:, cols(b)].astype(f32) for b in range(B)])

    def patch_forward(l):
        mix = dot(pw[l], xw[l])
        new = [xw[l, :, cols(b)].astype(f32) + (aa[l] * mix[:, cols(b)] + kk[l]) for b in range(B)]
        xt[l] = jnp.concatenate(new, axis=0).astype(bf16)

    def ffn_forward(l):
        x = xt[l]
        h, s = gelu_parts(dot(x, wus[l]) + bus[l])
        hid[l] = h
        slope[l] = s
        new = x.astype(f32) + (dot(h, wds[l]) + bdl[l])
        for b in range(B):
            xw[l + 1, :, cols(b)] = new[rows(b), :].astype(bf16)

    def ffn_up(l):
        h, s = gelu_parts(dot(xt[l], wus[l]) + bus[l])
        hid[l] = h
        slope[l] = s

    def back(l, weights):
        g = gt[l + 1]
        d = (dot(g, wds[l], 1, 1) * slope[l].astype(f32)).astype(bf16)
        dpre[...] = d
        new = g.astype(f32) + dot(d, wus[l], 1, 1)
        for b in range(B):
            gw[:, cols(b)] = new[rows(b), :].astype(bf16)
        back = dot(pw[l], gw[...], 0, 0)
        new = [gw[:, cols(b)].astype(f32) + aa[l] * back[:, cols(b)] for b in range(B)]
        gt[l] = jnp.concatenate(new, axis=0).astype(bf16)

        @pl.when(weights)
        def _():
            gdn[...] += jnp.sum(g.astype(f32), axis=0, keepdims=True)
            gx[...] += dot(xt[l].T, dpre[...])
            gd[...] += dot(gt[l + 1].T, hid[l])
            bup[...] += jnp.sum(dpre[...].astype(f32), axis=0, keepdims=True)
            scaled = jnp.concatenate([(gw[:, cols(b)].astype(f32) * aa[l]).astype(bf16) for b in range(B)], axis=1)
            gp[...] += dot(scaled, xw[l], 1, 1)
            mix = dot(pw[l], xw[l])
            for b in range(B):
                gb = gw[:, cols(b)].astype(f32)
                gsum[...] += gb
                sd[...] += jnp.sum(gb * mix[:, cols(b)], axis=0, keepdims=True)

    def step(t, carry):
        m = micro(t)
        other = lax.rem(m + half, M)
        mine = t < half
        slot = lax.rem(t, half)
        given = (sec == 3) & jnp.logical_not(mine)
        load(t, 0).wait()

        @pl.when(jnp.logical_not(given))
        def _():
            take(img, m)
            for b in range(B):
                xw[0, :, cols(b)] = stage[rows(b), :].astype(bf16)
            patch_forward(0)
            ffn_forward(0)

        @pl.when(sec == 0)
        def _():
            outs[m] = from_tall(xt[0])

        @pl.when(sec == 1)
        def _():
            outs[m] = from_wide(xw[1])

        @pl.when(given)
        def _():
            remote(xch.at[slot], xch.at[slot], slot).wait_recv()
            xt[1] = xch[slot]

        @pl.when((mine | (sec == 2)))
        def _():
            patch_forward(1)

        @pl.when((low & mine) | ((sec == 2) & mine))
        def _():
            ffn_up(1)

        @pl.when(sec == 2)
        def _():
            outs[m] = from_tall(xt[1])

            @pl.when(mine)
            def _():
                xch[slot] = xt[1]
                remote(xch.at[slot], xch.at[slot], slot).start()

        @pl.when(sec == 3)
        def _():
            ffn_forward(1)
            outs[m] = from_wide(xw[2])

        save(0, m).start()
        load(t, 1).wait()

        @pl.when(mine | (sec == 3))
        def _():
            take(og, m)
            gt[L] = stage[...].astype(bf16)
            back(1, (sec > 1) & mine)

            @pl.when(sec == 3)
            def _():
                gins[m] = from_wide(gw[...])

                @pl.when(mine)
                def _():
                    gins[M + slot] = from_tall(gt[1])
                    remote(gins.at[M + slot], gin_h.at[m], slot).start()

            @pl.when(sec == 2)
            def _():
                gins[m] = from_tall(gt[1])

            @pl.when(low)
            def _():
                back(0, low)
                gins[jnp.where(odd == 0, other, m)] = from_wide(gw[...])
                gins[jnp.where(odd == 0, m, other)] = from_tall(gt[0])
                remote(gins.at[other], gin_h.at[m], slot).start()

            save(1, m).start()
        return carry

    lax.fori_loop(0, M, step, 0)

    for l in range(L):
        @pl.when(own == l)
        def _():
            acol = jnp.broadcast_to(vec(ac, 2 * l + 1), (8, D)).T[:, 0:1]
            ccol = jnp.broadcast_to(vec(sh, 2 * l + 1), (8, D)).T[:, 0:1]
            scale1 = jnp.zeros((D, 1), f32)
            shift1 = jnp.zeros((D, 1), f32)
            for k in range(0, H, D):
                g = gx[:, k:k + D]
                w = wus[l, :, k:k + D].astype(f32)
                b = bup[:, k:k + D]
                grad_o[k:k + D, :] = (acol * g + ccol * b).astype(bf16)
                scale1 += jnp.sum(w * g, axis=1, keepdims=True)
                shift1 += jnp.sum(w * b, axis=1, keepdims=True)
            gain1 = jnp.zeros((1, D), f32)
            for k in range(0, H, D):
                g = gd[:, k:k + D].T
                gain1 += jnp.sum(g * wds[l, k:k + D, :].astype(f32), axis=0, keepdims=True)
                grad_o[H + k:H + k + D, :] = (g * vec(ls, 2 * l + 1)).astype(bf16)
            gain1 = gain1 / vec(ls, 2 * l + 1) + vec(bd, l) * gdn[...]
            scale1, shift1 = scale1 / acol, shift1 / acol
            both = jnp.broadcast_to(jnp.concatenate([scale1, shift1], axis=1), (D, 2)).T
            gs = gsum[...]
            lsrow, crow = vec(ls, 2 * l), vec(sh, 2 * l)
            wsum = jnp.sum(gs * rs[l], axis=0, keepdims=True)
            stage[0:PP, 0:PP] = gp[...] + jnp.sum(gs * (lsrow * crow), axis=1, keepdims=True)
            stage[0:PP, 256:257] = jnp.zeros((PP, 1), f32)
            stage[0:P, 256:257] = pbt[:, l:l + 1]
            psum = jnp.sum(gs * stage[0:PP, 256:257], axis=0, keepdims=True)
            offset = jnp.broadcast_to(jnp.sum(gs * lsrow, axis=1, keepdims=True), (PP, 8)).T[0:1, :]
            s_row = sd[...]
            extra = P + SMALL_ROWS

            def put(k, row):
                stage[P + k:P + k + 1, 0:row.shape[1]] = row
            stage[P:extra, :] = jnp.zeros((SMALL_ROWS, D), f32)
            put(ROW_SCALE, lsrow * s_row)
            put(ROW_SCALE + 1, both[0:1, :])
            put(ROW_SHIFT, lsrow * wsum)
            put(ROW_SHIFT + 1, both[1:2, :])
            put(ROW_GAIN, vec(ac, 2 * l) * s_row + crow * wsum + psum)
            put(ROW_GAIN + 1, gain1)
            put(ROW_OFFSET, offset[:, 0:P])
            for k in range(H // D):
                put(ROW_UPB + k, bup[:, k * D:(k + 1) * D])
            put(ROW_UPB + H // D, vec(ls, 2 * l + 1) * gdn[...])
            grad_o[2 * H:2 * H + extra, :] = stage[0:extra, :].astype(bf16)
    grad_o[2 * H + P + SMALL_ROWS:, :] = jnp.zeros((grad_o.shape[0] - 2 * H - P - SMALL_ROWS, D), bf16)
    for t in range(M):
        m = micro(t)
        save(0, m).wait()

        @pl.when((t < half) | (sec == 3))
        def _():
            save(1, m).wait()
    for t in range(half):
        @pl.when(sec == 2)
        def _():
            remote(xch.at[t], xch.at[t], t).wait_send()

        @pl.when(sec != 2)
        def _():
            remote(gins.at[t], gin_h.at[t], t).wait_send()

        @pl.when(sec != 3)
        def _():
            remote(gins.at[t], gin_h.at[t], t).wait_recv()


def compute_call(grad_rows, images, out_grad, live, ac, sh, ls, pw, pb, wu, bu, wd, bd):
    M, P, B, D = images.shape
    L, _, H = wu.shape
    PP = up_to(P, 8)
    R = B * PP
    vm = pl.BlockSpec(memory_space=pltpu.VMEM)
    hbm = pl.BlockSpec(memory_space=pl.ANY)
    return pl.pallas_call(
        compute_kernel,
        in_specs=[pl.BlockSpec(memory_space=pltpu.SMEM), hbm, hbm, vm, vm, vm, vm, vm, hbm, vm, hbm, vm],
        out_specs=[hbm, hbm, vm],
        out_shape=[jax.ShapeDtypeStruct(images.shape, bf16)] * 2 + [jax.ShapeDtypeStruct((grad_rows, D), bf16)],
        scratch_shapes=[
            pltpu.VMEM((M, P, B, D), bf16), pltpu.VMEM((M, P, B, D), bf16), pltpu.VMEM((M, P, B, D), bf16), pltpu.VMEM((M + M // 2, P, B, D), bf16),
            pltpu.VMEM((M // 2, R, D), bf16),
            pltpu.VMEM((L, PP, PP), bf16), pltpu.VMEM((L, PP, 1), f32), pltpu.VMEM((L, PP, D), f32), pltpu.VMEM((L, 1, D), f32), pltpu.VMEM((L, 1, D), f32),
            pltpu.VMEM((L, D, H), bf16), pltpu.VMEM((L, H, D), bf16), pltpu.VMEM((L, 1, H), f32),
            pltpu.VMEM((R, D), f32),
            pltpu.VMEM((L + 1, PP, B * D), bf16), pltpu.VMEM((L, R, D), bf16), pltpu.VMEM((PP, B * D), bf16), pltpu.VMEM((L + 1, R, D), bf16),
            pltpu.VMEM((L, R, H), bf16), pltpu.VMEM((L, R, H), bf16), pltpu.VMEM((R, H), bf16),
            pltpu.VMEM((D, H), f32), pltpu.VMEM((D, H), f32), pltpu.VMEM((PP, PP), f32), pltpu.VMEM((PP, D), f32),
            pltpu.VMEM((1, D), f32), pltpu.VMEM((1, H), f32), pltpu.VMEM((1, D), f32),
            pltpu.SemaphoreType.DMA((2, M)), pltpu.SemaphoreType.DMA((2, M)), pltpu.SemaphoreType.DMA((2,)),
            pltpu.SemaphoreType.DMA((M // 2,)), pltpu.SemaphoreType.DMA((M // 2,)),
        ],
        compiler_params=pltpu.CompilerParams(collective_id=2, has_side_effects=True, vmem_limit_bytes=60 * 2**20),
        name="chain",
    )(live, images, out_grad, ac, sh, ls, pw, pb, wu, bu, wd, bd)


def bits_of(n):
    return n.bit_length() - 1


def reduce_unit(n_dp):
    return 16 * n_dp


def reduce_kernel(n_dp, n_sec, g_ref, full, work, recv, send_sem, recv_sem, z_send, z_recv, g_send, g_recv):
    nb = bits_of(n_dp)
    half = full.shape[1] // 2
    unit = reduce_unit(n_dp)
    part_a = up_half = -(-(half // unit) // 2) * unit
    parts = [(0, part_a), (part_a, half - part_a)]
    parts = [p for p in parts if p[1] > 0]
    me = lax.axis_index("dp")
    sec = lax.axis_index("section")
    layer = sec // 2
    rest = list(range(1, nb))
    orders = [rest, rest[::-1]]
    bit = [(me // (1 << j)) % 2 for j in range(nb)]
    zbit = sec % 2

    def peer(j):
        return (me + (1 << j) - 2 * (1 << j) * bit[j], sec)

    zpeer = (me, sec + 1 - 2 * zbit)

    barrier = pltpu.get_barrier_semaphore()
    for j in range(nb):
        pl.semaphore_signal(barrier, inc=1, device_id=peer(j), device_id_type=pl.DeviceIdType.MESH)

    @pl.when(sec > 0)
    def _():
        pl.semaphore_signal(barrier, inc=1, device_id=(me, sec - 1), device_id_type=pl.DeviceIdType.MESH)

    @pl.when(sec < n_sec - 1)
    def _():
        pl.semaphore_signal(barrier, inc=1, device_id=(me, sec + 1), device_id_type=pl.DeviceIdType.MESH)

    pl.semaphore_wait(barrier, nb + jnp.where(sec > 0, 1, 0) + jnp.where(sec < n_sec - 1, 1, 0))

    def copy(src, dst, s, r, device):
        return pltpu.make_async_remote_copy(src_ref=src, dst_ref=dst, send_sem=s, recv_sem=r, device_id=device, device_id_type=pl.DeviceIdType.MESH)

    def rows(off, n):
        return pl.ds(pl.multiple_of(off, 16), n)

    base = bit[0] * half
    first = copy(g_ref.at[rows((1 - bit[0]) * half, half)], recv.at[pl.ds(0, half)], send_sem.at[0, 0], recv_sem.at[0, 0], peer(0))
    first.start()
    first.wait()
    work[...] = (g_ref[rows(base, half), :].astype(f32) + recv[0:half, :].astype(f32)).astype(bf16)

    place = [jnp.int32(off) for off, _ in parts]
    size = [n for _, n in parts]
    slot = half
    for t in range(nb):
        pending = []
        for k in range(len(parts)):
            n = size[k] // 2
            if t < nb - 1:
                b, device = bit[orders[k][t]], peer(orders[k][t])
            else:
                b, device = zbit, zpeer
            c = copy(work.at[rows(place[k] + (1 - b) * n, n)], recv.at[pl.ds(slot, n)], send_sem.at[k, t + 1], recv_sem.at[k, t + 1], device)
            c.start()
            pending.append((c, place[k] + b * n, n, slot))
            slot += n
        for k, (c, keep, n, at) in enumerate(pending):
            c.wait()
            total = work[rows(keep, n), :].astype(f32) + recv[at:at + n, :].astype(f32)
            if t < nb - 1:
                work[rows(keep, n), :] = total.astype(bf16)
            else:
                full[layer, rows(base + keep, n), :] = total.astype(bf16)
            place[k], size[k] = keep, n

    def piece(k, j):
        return full.at[j // 2, rows(base + place[k] + (j % 2 - zbit) * size[k], size[k])]

    def z_copies(k, j, d):
        target = sec + (1 if d == 0 else -1)
        return copy(piece(k, j), piece(k, j), z_send.at[k, d, abs_step(j)], z_recv.at[k, d, abs_step(j, 1)], (me, target))

    def abs_step(j, more=0):
        return more + jnp.where(j > sec, j - sec, sec - j)

    def z_send_item(dist, d):
        j = sec - dist if d == 0 else sec + dist
        target = sec + 1 if d == 0 else sec - 1
        ok = (j >= 0) & (target < n_sec) if d == 0 else (j < n_sec) & (target >= 0)

        @pl.when(ok)
        def _():
            for k in range(len(parts)):
                copy(piece(k, j), piece(k, j), z_send.at[k, d, dist], z_recv.at[k, d, dist], (me, target)).start()

    def z_wait_send(dist, d):
        j = sec - dist if d == 0 else sec + dist
        target = sec + 1 if d == 0 else sec - 1
        ok = (j >= 0) & (target < n_sec) if d == 0 else (j < n_sec) & (target >= 0)

        @pl.when(ok)
        def _():
            for k in range(len(parts)):
                copy(piece(k, j), piece(k, j), z_send.at[k, d, dist], z_recv.at[k, d, dist], (me, target)).wait_send()

    def z_wait_recv(dist, d):
        j = sec - dist - 1 if d == 0 else sec + dist + 1
        target = sec + 1 if d == 0 else sec - 1
        ok = (j >= 0) if d == 0 else (j < n_sec)

        @pl.when(ok)
        def _():
            for k in range(len(parts)):
                copy(piece(k, j), piece(k, j), z_send.at[k, d, dist], z_recv.at[k, d, dist], (me, sec)).wait_recv()

    def region(k, t):
        order = orders[k]
        off, n = jnp.int32(parts[k][0]), parts[k][1]
        for j in order[:len(order) - t]:
            n = n // 2
            off = off + bit[j] * n
        return off, n

    def g_copy(which, k, t, l):
        off, n = region(k, t)
        j = orders[k][len(orders[k]) - 1 - t]
        ref = full.at[l, rows(base + off, n)]
        return copy(ref, ref, g_send.at[which, k, t], g_recv.at[which, k, t], peer(j))

    def c_copy(which, l):
        ref = full.at[l, rows(base, half)]
        return copy(ref, ref, g_send.at[which, 0, nb - 1], g_recv.at[which, 0, nb - 1], peer(0))

    n_layer = n_sec // 2
    layers = [layer] + [(layer + i) % n_layer for i in range(1, n_layer)]
    steps = nb - 1
    for d in range(2):
        z_send_item(0, d)
    for d in range(2):
        z_wait_recv(0, d)
    for d in range(2):
        z_send_item(1, d)
    for k in range(len(parts)):
        g_copy(0, k, 0, layers[0]).start()
    for dist in range(1, n_sec - 1):
        for d in range(2):
            z_wait_recv(dist, d)
        if dist < n_sec - 2:
            for d in range(2):
                z_send_item(dist + 1, d)
        if dist <= steps:
            for k in range(len(parts)):
                g_copy(0, k, dist - 1, layers[0]).wait_recv()
                if dist < steps:
                    g_copy(0, k, dist, layers[0]).start()
    done = min(n_sec - 2, steps)
    for t in range(done, steps):
        for k in range(len(parts)):
            g_copy(0, k, t, layers[0]).wait_recv()
            if t + 1 < steps:
                g_copy(0, k, t + 1, layers[0]).start()
    c_copy(0, layers[0]).start()
    for w in range(1, n_layer):
        for t in range(steps):
            for k in range(len(parts)):
                g_copy(w, k, t, layers[w]).start()
            for k in range(len(parts)):
                g_copy(w, k, t, layers[w]).wait_recv()
        c_copy(w, layers[w]).start()
    for w in range(n_layer):
        c_copy(w, layers[w]).wait_recv()
    for w in range(n_layer):
        for t in range(steps):
            for k in range(len(parts)):
                g_copy(w, k, t, layers[w]).wait_send()
        c_copy(w, layers[w]).wait_send()
    for dist in range(n_sec - 1):
        for d in range(2):
            z_wait_send(dist, d)


def reduce_call(n_dp, n_sec, grads):
    rows, width = grads.shape
    nb = bits_of(n_dp)
    vm = pl.BlockSpec(memory_space=pltpu.VMEM)
    return pl.pallas_call(
        functools.partial(reduce_kernel, n_dp, n_sec),
        in_specs=[vm],
        out_specs=vm,
        out_shape=jax.ShapeDtypeStruct((n_sec // 2, rows, width), bf16),
        scratch_shapes=[
            pltpu.VMEM((rows // 2, width), bf16), pltpu.VMEM((rows, width), bf16),
            pltpu.SemaphoreType.DMA((2, nb + 1)), pltpu.SemaphoreType.DMA((2, nb + 1)),
            pltpu.SemaphoreType.DMA((2, 2, n_sec)), pltpu.SemaphoreType.DMA((2, 2, n_sec)),
            pltpu.SemaphoreType.DMA((n_sec // 2, 2, nb)), pltpu.SemaphoreType.DMA((n_sec // 2, 2, nb)),
        ],
        compiler_params=pltpu.CompilerParams(collective_id=1, has_side_effects=True, vmem_limit_bytes=48 * 2**20),
        name="reduce",
    )(grads)


def finish_kernel(P, full, scale_o, shift_o, gain_o, pw_o, off_o, up_o, upb_o, down_o, dnb_o):
    L = pw_o.shape[1]
    D, H = up_o.shape[1:]
    step = pl.program_id(0)
    for k in range(0, H, D):
        up_o[0, :, k:k + D] = full[0, k:k + D, :].astype(f32)
    down_o[0] = full[0, H:2 * H, :].astype(f32)
    tail = full[0, 2 * H:2 * H + up_to(P + SMALL_ROWS, 16), :].astype(f32)
    small = tail[P:P + SMALL_ROWS, :]
    for l in range(L):
        @pl.when(step == l)
        def _():
            pw_o[:, l, :] = tail[0:P, 0:P]
            for out, row in ((scale_o, ROW_SCALE), (shift_o, ROW_SHIFT), (gain_o, ROW_GAIN)):
                out[2 * l:2 * l + 2, :] = small[row:row + 2, :]
            off_o[l:l + 1, :] = small[ROW_OFFSET:ROW_OFFSET + 1, 0:P]
            for k in range(H // D):
                upb_o[l:l + 1, k * D:(k + 1) * D] = small[ROW_UPB + k:ROW_UPB + k + 1, :]
            dnb_o[l:l + 1, :] = small[ROW_UPB + H // D:ROW_UPB + H // D + 1, :]


def finish_call(full, P, H):
    L, rows, D = full.shape
    const = lambda *shape: pl.BlockSpec(shape, lambda i: (0,) * len(shape))
    return pl.pallas_call(
        functools.partial(finish_kernel, P),
        grid=(L,),
        in_specs=[pl.BlockSpec((1, rows, D), lambda i: (i, 0, 0))],
        out_specs=[const(2 * L, D), const(2 * L, D), const(2 * L, D), const(P, L, P), const(L, P),
                   pl.BlockSpec((1, D, H), lambda i: (i, 0, 0)), const(L, H), pl.BlockSpec((1, H, D), lambda i: (i, 0, 0)), const(L, D)],
        out_shape=[jax.ShapeDtypeStruct(s, f32) for s in ((2 * L, D), (2 * L, D), (2 * L, D), (P, L, P), (L, P), (L, D, H), (L, H), (L, H, D), (L, D))],
        compiler_params=pltpu.CompilerParams(vmem_limit_bytes=40 * 2**20),
        name="finish",
    )(full)


def shards(n_dp, n_sec, images, out_grad, padding, affine_scale, affine_shift, layer_scale, patch_weight, patch_bias, up_weight, up_bias, down_weight, down_bias):
    n_patch, width = images.shape[2:]
    hidden = up_weight.shape[2]
    grad_rows = up_to(2 * hidden + n_patch + SMALL_ROWS, 2 * reduce_unit(n_dp))
    outputs, in_grads, grads = compute_call(
        grad_rows,
        images.transpose(0, 2, 1, 3), out_grad.transpose(0, 2, 1, 3), padding.T,
        affine_scale, affine_shift, layer_scale, patch_weight.transpose(1, 0, 2), patch_bias,
        up_weight, up_bias, down_weight, down_bias,
    )
    full = reduce_call(n_dp, n_sec, grads)
    scale, shift, gain, slopes, offset, up, upb, down, dnb = finish_call(full, n_patch, hidden)
    native = lambda a: a.transpose(0, 2, 1, 3)[None]
    return native(outputs), native(in_grads), scale, shift, gain, slopes.transpose(1, 0, 2), offset, up, upb, down, dnb


def solution(mesh):
    split = P(None, "dp", None, None)
    return jax.shard_map(
        functools.partial(shards, mesh.shape["dp"], mesh.shape["section"]),
        mesh=mesh,
        in_specs=(split, split, P(None, "dp")) + (P(),) * 9,
        out_specs=(P("section", None, "dp", None, None),) * 2 + (P(),) * 9,
        check_vma=False,
    )
```

```python
import functools

import jax
import jax.numpy as jnp
from jax import lax
from jax.experimental import pallas as pl
from jax.experimental.pallas import tpu as pltpu
from jax.sharding import PartitionSpec as P

f32, bf16 = jnp.float32, jnp.bfloat16
C0 = 0.7978845608028654
C1 = 0.044715
SMALL_ROWS = 12
ROW_SCALE, ROW_SHIFT, ROW_GAIN, ROW_OFFSET, ROW_UPB = 0, 2, 4, 6, 7


def dot(a, b, ca=1, cb=0):
    return lax.dot_general(a, b, (((ca,), (cb,)), ((), ())), preferred_element_type=f32)


def up_to(n, k):
    return -(-n // k) * k


def gelu_parts(pre):
    pre = pre.astype(bf16)
    c0, c01, c03 = bf16(C0), bf16(C0 * C1), bf16(3 * C0 * C1)
    half, one = bf16(0.5), bf16(1.0)
    square = pre * pre
    t = jnp.tanh(pre * (c0 + c01 * square))
    hx = half * pre
    return hx + hx * t, (half + half * t) + hx * (one - t * t) * (c0 + c03 * square)


def bits_of(n):
    return n.bit_length() - 1


def reduce_unit(n_dp):
    return 16 * n_dp


def reduce_parts(half, unit, most=4):
    units = half // unit
    count = min(most, units)
    ends = [units * (k + 1) // count for k in range(count)]
    starts = [0] + ends[:-1]
    return [(a * unit, (b - a) * unit) for a, b in zip(starts, ends)]


def chain_kernel(n_dp, n_sec, live_ref, img_h, og_h, ac, sh, ls, pw_in, pb_in, wu_h, bu, wd_h, bd, out_h, gin_h, full,
                 img, og, xch, pw, rs, kk, aa, bdl, wus, wds, bus, stage, xw, xt, gw, gt, hid, slope, dpre,
                 gx, gd, gp, gsum, sd, bup, gdn, grad_o, work, recv,
                 in_sem, out_sem, w_sem, pair_send, pair_recv, send_sem, recv_sem, z_send, z_recv, g_send, g_recv):
    M, P, B, D = out_h.shape
    L, _, H = wus.shape
    PP = pw.shape[1]
    R = B * PP
    RC = R // 2 if R % 32 == 0 else R
    HC = H // 2 if H % 512 == 0 else H
    me, sec = lax.axis_index("dp"), lax.axis_index("section")
    own, odd = sec // 2, sec % 2
    low = sec < 2
    partner = (me, sec + 1 - 2 * odd)
    half_m = M // 2
    nb = bits_of(n_dp)
    half = full.shape[1] // 2
    parts = reduce_parts(half, reduce_unit(n_dp))
    n_part = len(parts)
    every = range(n_part)
    rest = list(range(1, nb))
    orders = [rest if k % 2 == 0 else rest[::-1] for k in every]
    bit = [(me // (1 << j)) % 2 for j in range(nb)]
    zbit = odd
    base = bit[0] * half

    def peer(j):
        return (me + (1 << j) - 2 * (1 << j) * bit[j], sec)

    def signal(device):
        pl.semaphore_signal(barrier, inc=1, device_id=device, device_id_type=pl.DeviceIdType.MESH)

    def copy(src, dst, s, r, device):
        return pltpu.make_async_remote_copy(src_ref=src, dst_ref=dst, send_sem=s, recv_sem=r, device_id=device, device_id_type=pl.DeviceIdType.MESH)

    def rows(b):
        return slice(b * PP, (b + 1) * PP)

    def span(off, n):
        return pl.ds(pl.multiple_of(off, 128 if n % 128 == 0 and n == HC else 16), n)

    def cols(b):
        return slice(b * D, (b + 1) * D)

    def vec(ref, k):
        return ref[k:k + 1, :].astype(f32)

    def micro(t):
        return lax.rem(t + half_m * odd, M)

    def needs(t, which):
        return (t < half_m) | ((sec == 3) if which else (sec < 3))

    def load(t, which):
        m = micro(t)
        return pltpu.make_async_copy((img_h, og_h)[which].at[m], (img, og)[which].at[m], in_sem.at[which, m])

    def save(which, m):
        return pltpu.make_async_copy((img, og)[which].at[m], (out_h, gin_h)[which].at[m], out_sem.at[which, m])

    def pair(src, dst, t):
        return copy(src, dst, pair_send.at[t], pair_recv.at[t], partner)

    barrier = pltpu.get_barrier_semaphore()
    for j in range(nb):
        signal(peer(j))

    @pl.when(sec > 0)
    def _():
        signal((me, sec - 1))

    @pl.when(sec < n_sec - 1)
    def _():
        signal((me, sec + 1))

    load(0, 0).start()
    w_up = pltpu.make_async_copy(wu_h, wus, w_sem.at[0])
    w_down = pltpu.make_async_copy(wd_h, wds, w_sem.at[1])
    w_up.start()
    w_down.start()
    load(0, 1).start()
    for t in range(1, M):
        for which in range(2):
            @pl.when(needs(t, which))
            def _():
                load(t, which).start()

    pw[...] = jnp.zeros_like(pw)
    pbt = jnp.concatenate([pb_in[...].astype(f32), jnp.zeros((8 - L, P), f32)], axis=0).T
    stage[...] = jnp.zeros_like(stage)
    for l in range(L):
        pw[l, :P, :P] = pw_in[:, l, :]
        rs[l] = jnp.sum(pw[l].astype(f32), axis=1, keepdims=True)
        stage[0:P, l:l + 1] = pbt[:, l:l + 1]
        kk[l] = vec(ls, 2 * l) * (vec(sh, 2 * l) * rs[l] + stage[0:PP, l:l + 1])
        aa[l] = vec(ac, 2 * l) * vec(ls, 2 * l)
        bdl[l] = vec(bd, l) * vec(ls, 2 * l + 1)
    stage[0:PP, 0:128] = jnp.zeros((PP, 128), f32)
    for r in (gx, gd, gp, gsum, sd, bup, gdn):
        r[...] = jnp.zeros_like(r)
    w_up.wait()
    w_down.wait()
    for l in range(L):
        acol = jnp.broadcast_to(vec(ac, 2 * l + 1), (8, D)).T[:, 0:1]
        shift8 = jnp.broadcast_to(vec(sh, 2 * l + 1), (8, D)).astype(bf16)
        for k in range(0, H, D):
            bus[l, :, k:k + D] = dot(shift8, wus[l, :, k:k + D])[0:1, :] + bu[l:l + 1, k:k + D].astype(f32)
            wus[l, :, k:k + D] = (wus[l, :, k:k + D].astype(f32) * acol).astype(bf16)
            wds[l, k:k + D, :] = (wds[l, k:k + D, :].astype(f32) * vec(ls, 2 * l + 1)).astype(bf16)
    pl.semaphore_wait(barrier, nb + jnp.where(sec > 0, 1, 0) + jnp.where(sec < n_sec - 1, 1, 0))

    def take(ref, m):
        v = jnp.swapaxes(ref[m].astype(f32), 0, 1)
        for b in range(B):
            stage[b * PP:b * PP + P, :] = v[b] * live_ref[b, m].astype(f32)
            stage[b * PP + P:(b + 1) * PP, :] = jnp.zeros((PP - P, D), f32)

    def turned(pieces):
        return jnp.swapaxes(jnp.stack([p[0:P, :] for p in pieces], axis=0), 0, 1).astype(bf16)

    def from_tall(value):
        value = value.astype(f32)
        return turned([value[rows(b), :] for b in range(B)])

    def from_wide(value):
        return turned([value[:, cols(b)].astype(f32) for b in range(B)])

    def patch_forward(l):
        mix = dot(pw[l], xw[l])
        new = [xw[l, :, cols(b)].astype(f32) + (aa[l] * mix[:, cols(b)] + kk[l]) for b in range(B)]
        xt[l] = jnp.concatenate(new, axis=0).astype(bf16)

    def ffn_forward(l):
        x = xt[l]
        h, s = gelu_parts(dot(x, wus[l]) + bus[l])
        hid[l] = h
        slope[l] = s
        new = x.astype(f32) + (dot(h, wds[l]) + bdl[l])
        for b in range(B):
            xw[l + 1, :, cols(b)] = new[rows(b), :].astype(bf16)

    def ffn_up(l):
        h, s = gelu_parts(dot(xt[l], wus[l]) + bus[l])
        hid[l] = h
        slope[l] = s

    def ffn_back(l):
        def piece_back(i, carry):
            q = span(i * RC, RC)
            g = gt[l + 1, q, :]
            d = (dot(g, wds[l], 1, 1) * slope[l, q, :].astype(f32)).astype(bf16)
            dpre[q, :] = d
            stage[q, :] = g.astype(f32) + dot(d, wus[l], 1, 1)
            return carry

        lax.fori_loop(0, R // RC, piece_back, 0)
        for b in range(B):
            gw[:, cols(b)] = stage[rows(b), :].astype(bf16)

    def back(l):
        ffn_back(l)
        moved = dot(pw[l], gw[...], 0, 0)
        new = [gw[:, cols(b)].astype(f32) + aa[l] * moved[:, cols(b)] for b in range(B)]
        gt[l] = jnp.concatenate(new, axis=0).astype(bf16)

        @pl.when(own == l)
        def _():
            gdn[...] += jnp.sum(gt[l + 1].astype(f32), axis=0, keepdims=True)
            x_t, g_t = xt[l].T, gt[l + 1].T

            def weight_piece(i, carry):
                q = span(i * HC, HC)
                gx[:, q] += dot(x_t, dpre[:, q])
                gd[:, q] += dot(g_t, hid[l, :, q])
                bup[:, q] += jnp.sum(dpre[:, q].astype(f32), axis=0, keepdims=True)
                return carry

            lax.fori_loop(0, H // HC, weight_piece, 0)
            scaled = jnp.concatenate([(gw[:, cols(b)].astype(f32) * aa[l]).astype(bf16) for b in range(B)], axis=1)
            gp[...] += dot(scaled, xw[l], 1, 1)
            mix = dot(pw[l], xw[l])
            for b in range(B):
                gb = gw[:, cols(b)].astype(f32)
                gsum[...] += gb
                sd[...] += jnp.sum(gb * mix[:, cols(b)], axis=0, keepdims=True)

    def read_images(t, m):
        load(t, 0).wait()
        take(img, m)
        for b in range(B):
            xw[0, :, cols(b)] = stage[rows(b), :].astype(bf16)

    def whole(t, carry):
        m = micro(t)
        other = lax.rem(m + half_m, M)
        read_images(t, m)
        patch_forward(0)
        ffn_forward(0)

        @pl.when(sec == 0)
        def _():
            img[m] = from_tall(xt[0])

        @pl.when(sec == 1)
        def _():
            img[m] = from_wide(xw[1])

        patch_forward(1)

        @pl.when(sec == 2)
        def _():
            img[m] = from_tall(xt[1])
            xch[t] = xt[1]
            pair(xch.at[t], xch.at[t], t).start()

        ffn_up(1)

        @pl.when(sec == 3)
        def _():
            new = xt[1].astype(f32) + (dot(hid[1], wds[1]) + bdl[1])
            img[m] = turned([new[rows(b), :] for b in range(B)])

        save(0, m).start()
        load(t, 1).wait()
        take(og, m)
        gt[L] = stage[...].astype(bf16)

        def half_back(i, carry):
            l = L - 1 - i
            back(l)

            @pl.when(sec == 3)
            def _():
                og[m] = from_wide(gw[...])
                og[M + t] = from_tall(gt[l])
                pair(og.at[M + t], gin_h.at[m], t).start()

            @pl.when(sec == 2)
            def _():
                og[m] = from_tall(gt[l])

            @pl.when(low & (l == 0))
            def _():
                og[jnp.where(odd == 0, other, m)] = from_wide(gw[...])
                og[jnp.where(odd == 0, m, other)] = from_tall(gt[l])
                pair(og.at[other], gin_h.at[m], t).start()
            return carry

        lax.fori_loop(0, jnp.where(low, L, 1), half_back, 0)
        save(1, m).start()
        return carry

    lax.fori_loop(0, half_m, whole, 0)

    for l in range(L):
        @pl.when(own == l)
        def _():
            acol = jnp.broadcast_to(vec(ac, 2 * l + 1), (8, D)).T[:, 0:1]
            ccol = jnp.broadcast_to(vec(sh, 2 * l + 1), (8, D)).T[:, 0:1]
            scale1 = jnp.zeros((D, 1), f32)
            shift1 = jnp.zeros((D, 1), f32)
            for k in range(0, H, D):
                g = gx[:, k:k + D]
                w = wus[l, :, k:k + D].astype(f32)
                b = bup[:, k:k + D]
                grad_o[k:k + D, :] = (acol * g + ccol * b).astype(bf16)
                scale1 += jnp.sum(w * g, axis=1, keepdims=True)
                shift1 += jnp.sum(w * b, axis=1, keepdims=True)
            gain1 = jnp.zeros((1, D), f32)
            for k in range(0, H, D):
                g = gd[:, k:k + D].T
                gain1 += jnp.sum(g * wds[l, k:k + D, :].astype(f32), axis=0, keepdims=True)
                grad_o[H + k:H + k + D, :] = (g * vec(ls, 2 * l + 1)).astype(bf16)
            gain1 = gain1 / vec(ls, 2 * l + 1) + vec(bd, l) * gdn[...]
            scale1, shift1 = scale1 / acol, shift1 / acol
            both = jnp.broadcast_to(jnp.concatenate([scale1, shift1], axis=1), (D, 2)).T
            gs = gsum[...]
            lsrow, crow = vec(ls, 2 * l), vec(sh, 2 * l)
            wsum = jnp.sum(gs * rs[l], axis=0, keepdims=True)
            stage[0:PP, 0:PP] = gp[...] + jnp.sum(gs * (lsrow * crow), axis=1, keepdims=True)
            stage[0:PP, 256:257] = jnp.zeros((PP, 1), f32)
            stage[0:P, 256:257] = pbt[:, l:l + 1]
            psum = jnp.sum(gs * stage[0:PP, 256:257], axis=0, keepdims=True)
            offset = jnp.broadcast_to(jnp.sum(gs * lsrow, axis=1, keepdims=True), (PP, 8)).T[0:1, :]
            s_row = sd[...]
            extra = P + SMALL_ROWS

            def put(k, row):
                stage[P + k:P + k + 1, 0:row.shape[1]] = row
            stage[P:extra, :] = jnp.zeros((SMALL_ROWS, D), f32)
            put(ROW_SCALE, lsrow * s_row)
            put(ROW_SCALE + 1, both[0:1, :])
            put(ROW_SHIFT, lsrow * wsum)
            put(ROW_SHIFT + 1, both[1:2, :])
            put(ROW_GAIN, vec(ac, 2 * l) * s_row + crow * wsum + psum)
            put(ROW_GAIN + 1, gain1)
            put(ROW_OFFSET, offset[:, 0:P])
            for k in range(H // D):
                put(ROW_UPB + k, bup[:, k * D:(k + 1) * D])
            put(ROW_UPB + H // D, vec(ls, 2 * l + 1) * gdn[...])
            grad_o[2 * H:2 * H + extra, :] = stage[0:extra, :].astype(bf16)
    grad_o[2 * H + P + SMALL_ROWS:, :] = jnp.zeros((grad_o.shape[0] - 2 * H - P - SMALL_ROWS, D), bf16)

    def at_step(k, t):
        off, n = jnp.int32(parts[k][0]), parts[k][1]
        for j in orders[k][:t - 1]:
            n = n // 2
            off = off + bit[j] * n
        if t > nb:
            n = n // 2
            off = off + zbit * n
        return off, n

    def exchange(k, t):
        if t == 0:
            off, n = parts[k]
            return copy(grad_o.at[span((1 - bit[0]) * half + off, n)], recv.at[pl.ds(2 * off, n)], send_sem.at[k, 0], recv_sem.at[k, 0], peer(0)), 2 * off
        off, n = at_step(k, t)
        b, device = (bit[orders[k][t - 1]], peer(orders[k][t - 1])) if t < nb else (zbit, partner)
        slot = 2 * parts[k][0] + sum(parts[k][1] >> u for u in range(t))
        return copy(work.at[span(off + (1 - b) * (n // 2), n // 2)], recv.at[pl.ds(slot, n // 2)], send_sem.at[k, t], recv_sem.at[k, t], device), slot

    def add_step(t):
        for k in every:
            c, slot = exchange(k, t)
            c.wait_recv()
            off, n = at_step(k, t + 1)
            piece_rows = parts[k][1] >> nb

            def add(i, carry):
                at = i * piece_rows
                mine = grad_o[span(base + off + at, piece_rows), :] if t == 0 else work[span(off + at, piece_rows), :]
                total = (mine.astype(f32) + recv[span(slot + at, piece_rows), :].astype(f32)).astype(bf16)
                if t < nb:
                    work[span(off + at, piece_rows), :] = total
                else:
                    full[own, span(base + off + at, piece_rows), :] = total
                return carry

            lax.fori_loop(0, n // piece_rows, add, 0)
            if t < nb:
                exchange(k, t + 1)[0].start()
            else:
                for d in range(2):
                    z_send_item(0, d, k)

    place, size = zip(*[at_step(k, nb + 1) for k in every])

    def piece(k, j):
        return full.at[j // 2, span(base + place[k] + (j % 2 - zbit) * size[k], size[k])]

    def z_case(dist, d):
        j, target = (sec - dist, sec + 1) if d == 0 else (sec + dist, sec - 1)
        return j, target, ((j >= 0) & (target < n_sec)) if d == 0 else ((j < n_sec) & (target >= 0))

    def z_copy(dist, d, k, j, target):
        return copy(piece(k, j), piece(k, j), z_send.at[k, d, dist], z_recv.at[k, d, dist], (me, target))

    def z_send_item(dist, d, k):
        j, target, ok = z_case(dist, d)

        @pl.when(ok)
        def _():
            z_copy(dist, d, k, j, target).start()

    def z_wait_send(dist, d, k):
        j, target, ok = z_case(dist, d)

        @pl.when(ok)
        def _():
            z_copy(dist, d, k, j, target).wait_send()

    def z_wait_recv(dist, d, k):
        j = sec - dist - 1 if d == 0 else sec + dist + 1

        @pl.when((j >= 0) & (j < n_sec))
        def _():
            z_copy(dist, d, k, j, sec).wait_recv()

    def region(k, t):
        order = orders[k]
        off, n = jnp.int32(parts[k][0]), parts[k][1]
        for j in order[:len(order) - t]:
            n = n // 2
            off = off + bit[j] * n
        return off, n

    def g_copy(w, k, t, l):
        off, n = region(k, t)
        ref = full.at[l, span(base + off, n)]
        return copy(ref, ref, g_send.at[w, k, t], g_recv.at[w, k, t], peer(orders[k][len(orders[k]) - 1 - t]))

    def c_copy(w, k, l):
        ref = full.at[l, span(base + parts[k][0], parts[k][1])]
        return copy(ref, ref, g_send.at[w, k, nb - 1], g_recv.at[w, k, nb - 1], peer(0))

    layers = [own] + [(own + i) % L for i in range(1, L)]
    steps = nb - 1

    def gather(w, t):
        for k in every:
            g_copy(w, k, t, layers[w]).wait_recv()
            if t + 1 < steps:
                g_copy(w, k, t + 1, layers[w]).start()
            else:
                c_copy(w, k, layers[w]).start()

    def line(dist):
        for k in every:
            for d in range(2):
                z_wait_recv(dist, d, k)
            if dist < n_sec - 2:
                for d in range(2):
                    z_send_item(dist + 1, d, k)
            if dist == 0:
                g_copy(0, k, 0, layers[0]).start()
            if dist == n_sec - 2:
                for w in range(1, L):
                    g_copy(w, k, 0, layers[w]).start()

    waves = [functools.partial(add_step, t) for t in range(nb + 1)]
    waves.append(functools.partial(line, 0))
    for dist in range(1, n_sec - 1):
        waves.append(functools.partial(line, dist))
        if dist <= steps:
            waves.append(functools.partial(gather, 0, dist - 1))
    for t in range(min(n_sec - 2, steps), steps):
        waves.append(functools.partial(gather, 0, t))
    for w in range(1, L):
        for t in range(steps):
            waves.append(functools.partial(gather, w, t))

    def rest_forward(t):
        m = micro(t)

        @pl.when(sec < 3)
        def _():
            read_images(t, m)
            patch_forward(0)

        @pl.when(sec == 0)
        def _():
            img[m] = from_tall(xt[0])

        @pl.when(sec == 3)
        def _():
            slot = t - half_m
            pair(xch.at[slot], xch.at[slot], slot).wait_recv()
            xt[1] = xch[slot]

        @pl.when(sec > 0)
        def _():
            l = jnp.where(sec == 3, 1, 0)
            ffn_forward(l)

            @pl.when(sec != 2)
            def _():
                img[m] = from_wide(xw[l + 1])

        @pl.when(sec == 2)
        def _():
            patch_forward(1)
            img[m] = from_tall(xt[1])

        save(0, m).start()

    def rest_backward(t):
        m = micro(t)

        @pl.when(sec == 3)
        def _():
            load(t, 1).wait()
            take(og, m)
            gt[L] = stage[...].astype(bf16)
            ffn_back(L - 1)
            og[m] = from_wide(gw[...])
            save(1, m).start()

    for k in every:
        exchange(k, 0)[0].start()
    beside = 2 * (M - half_m)

    def rest_step(t, carry):
        for i, piece_of_work in enumerate((rest_forward, rest_backward)):
            piece_of_work(t)
            for n in range(i, min(beside, len(waves)), 2):
                @pl.when(t == half_m + n // 2)
                def _():
                    waves[n]()
        return carry

    lax.fori_loop(half_m, M, rest_step, 0)
    for wave in waves[beside:]:
        wave()
    for w in range(L):
        for k in every:
            c_copy(w, k, layers[w]).wait_recv()

    for k in every:
        for t in range(nb + 1):
            exchange(k, t)[0].wait_send()
        for w in range(L):
            for t in range(steps):
                g_copy(w, k, t, layers[w]).wait_send()
            c_copy(w, k, layers[w]).wait_send()
        for dist in range(n_sec - 1):
            for d in range(2):
                z_wait_send(dist, d, k)
    for t in range(M):
        m = micro(t)
        save(0, m).wait()

        @pl.when((t < half_m) | (sec == 3))
        def _():
            save(1, m).wait()
    for t in range(half_m):
        @pl.when(sec == 2)
        def _():
            pair(xch.at[t], xch.at[t], t).wait_send()

        @pl.when(sec != 2)
        def _():
            pair(og.at[t], gin_h.at[t], t).wait_send()

        @pl.when(sec != 3)
        def _():
            pair(og.at[t], gin_h.at[t], t).wait_recv()


def chain_call(n_dp, n_sec, images, out_grad, live, ac, sh, ls, pw, pb, wu, bu, wd, bd):
    M, P, B, D = images.shape
    L, _, H = wu.shape
    PP = up_to(P, 8)
    R = B * PP
    total = up_to(2 * H + P + SMALL_ROWS, 2 * reduce_unit(n_dp))
    nb = bits_of(n_dp)
    n_part = len(reduce_parts(total // 2, reduce_unit(n_dp)))
    vm = pl.BlockSpec(memory_space=pltpu.VMEM)
    hbm = pl.BlockSpec(memory_space=pl.ANY)
    sem = pltpu.SemaphoreType.DMA
    return pl.pallas_call(
        functools.partial(chain_kernel, n_dp, n_sec),
        in_specs=[pl.BlockSpec(memory_space=pltpu.SMEM), hbm, hbm, vm, vm, vm, vm, vm, hbm, vm, hbm, vm],
        out_specs=[hbm, hbm, vm],
        out_shape=[jax.ShapeDtypeStruct(images.shape, bf16)] * 2 + [jax.ShapeDtypeStruct((L, total, D), bf16)],
        scratch_shapes=[
            pltpu.VMEM((M, P, B, D), bf16), pltpu.VMEM((M + M // 2, P, B, D), bf16), pltpu.VMEM((M // 2, R, D), bf16),
            pltpu.VMEM((L, PP, PP), bf16), pltpu.VMEM((L, PP, 1), f32), pltpu.VMEM((L, PP, D), f32), pltpu.VMEM((L, 1, D), f32), pltpu.VMEM((L, 1, D), f32),
            pltpu.VMEM((L, D, H), bf16), pltpu.VMEM((L, H, D), bf16), pltpu.VMEM((L, 1, H), f32),
            pltpu.VMEM((R, D), f32),
            pltpu.VMEM((L + 1, PP, B * D), bf16), pltpu.VMEM((L, R, D), bf16), pltpu.VMEM((PP, B * D), bf16), pltpu.VMEM((L + 1, R, D), bf16),
            pltpu.VMEM((L, R, H), bf16), pltpu.VMEM((L, R, H), bf16), pltpu.VMEM((R, H), bf16),
            pltpu.VMEM((D, H), f32), pltpu.VMEM((D, H), f32), pltpu.VMEM((PP, PP), f32), pltpu.VMEM((PP, D), f32),
            pltpu.VMEM((1, D), f32), pltpu.VMEM((1, H), f32), pltpu.VMEM((1, D), f32),
            pltpu.VMEM((total, D), bf16), pltpu.VMEM((total // 2, D), bf16), pltpu.VMEM((total, D), bf16),
            sem((2, M)), sem((2, M)), sem((2,)), sem((M // 2,)), sem((M // 2,)),
            sem((n_part, nb + 1)), sem((n_part, nb + 1)), sem((n_part, 2, n_sec)), sem((n_part, 2, n_sec)),
            sem((L, n_part, nb)), sem((L, n_part, nb)),
        ],
        compiler_params=pltpu.CompilerParams(collective_id=1, has_side_effects=True, vmem_limit_bytes=62 * 2**20),
        name="chain",
    )(live, images, out_grad, ac, sh, ls, pw, pb, wu, bu, wd, bd)


def finish_kernel(P, full, scale_o, shift_o, gain_o, pw_o, off_o, up_o, upb_o, down_o, dnb_o):
    L = pw_o.shape[1]
    D, H = up_o.shape[1:]
    step = pl.program_id(0)
    for k in range(0, H, D):
        up_o[0, :, k:k + D] = full[0, k:k + D, :].astype(f32)
    down_o[0] = full[0, H:2 * H, :].astype(f32)
    tail = full[0, 2 * H:2 * H + up_to(P + SMALL_ROWS, 16), :].astype(f32)
    small = tail[P:P + SMALL_ROWS, :]
    for l in range(L):
        @pl.when(step == l)
        def _():
            pw_o[:, l, :] = tail[0:P, 0:P]
            for out, row in ((scale_o, ROW_SCALE), (shift_o, ROW_SHIFT), (gain_o, ROW_GAIN)):
                out[2 * l:2 * l + 2, :] = small[row:row + 2, :]
            off_o[l:l + 1, :] = small[ROW_OFFSET:ROW_OFFSET + 1, 0:P]
            for k in range(H // D):
                upb_o[l:l + 1, k * D:(k + 1) * D] = small[ROW_UPB + k:ROW_UPB + k + 1, :]
            dnb_o[l:l + 1, :] = small[ROW_UPB + H // D:ROW_UPB + H // D + 1, :]


def finish_call(full, P, H):
    L, rows, D = full.shape
    const = lambda *shape: pl.BlockSpec(shape, lambda i: (0,) * len(shape))
    return pl.pallas_call(
        functools.partial(finish_kernel, P),
        grid=(L,),
        in_specs=[pl.BlockSpec((1, rows, D), lambda i: (i, 0, 0))],
        out_specs=[const(2 * L, D), const(2 * L, D), const(2 * L, D), const(P, L, P), const(L, P),
                   pl.BlockSpec((1, D, H), lambda i: (i, 0, 0)), const(L, H), pl.BlockSpec((1, H, D), lambda i: (i, 0, 0)), const(L, D)],
        out_shape=[jax.ShapeDtypeStruct(s, f32) for s in ((2 * L, D), (2 * L, D), (2 * L, D), (P, L, P), (L, P), (L, D, H), (L, H), (L, H, D), (L, D))],
        compiler_params=pltpu.CompilerParams(vmem_limit_bytes=40 * 2**20),
        name="finish",
    )(full)


def shards(n_dp, n_sec, images, out_grad, padding, affine_scale, affine_shift, layer_scale, patch_weight, patch_bias, up_weight, up_bias, down_weight, down_bias):
    outputs, in_grads, full = chain_call(
        n_dp, n_sec,
        images.transpose(0, 2, 1, 3), out_grad.transpose(0, 2, 1, 3), padding.T,
        affine_scale, affine_shift, layer_scale, patch_weight.transpose(1, 0, 2), patch_bias,
        up_weight, up_bias, down_weight, down_bias,
    )
    scale, shift, gain, slopes, offset, up, upb, down, dnb = finish_call(full, images.shape[2], up_weight.shape[2])
    native = lambda a: a.transpose(0, 2, 1, 3)[None]
    return native(outputs), native(in_grads), scale, shift, gain, slopes.transpose(1, 0, 2), offset, up, upb, down, dnb


def solution(mesh):
    split = P(None, "dp", None, None)
    return jax.shard_map(
        functools.partial(shards, mesh.shape["dp"], mesh.shape["section"]),
        mesh=mesh,
        in_specs=(split, split, P(None, "dp")) + (P(),) * 9,
        out_specs=(P("section", None, "dp", None, None),) * 2 + (P(),) * 9,
        check_vma=False,
    )
```

```python
import functools

import jax
import jax.numpy as jnp
from jax import lax
from jax.experimental import pallas as pl
from jax.experimental.pallas import tpu as pltpu
from jax.sharding import PartitionSpec as P

f32, bf16 = jnp.float32, jnp.bfloat16
C0 = 0.7978845608028654
C1 = 0.044715
SMALL_ROWS = 12
ROW_SCALE, ROW_SHIFT, ROW_GAIN, ROW_OFFSET, ROW_UPB = 0, 2, 4, 6, 7


def dot(a, b, ca=1, cb=0):
    return lax.dot_general(a, b, (((ca,), (cb,)), ((), ())), preferred_element_type=f32)


def up_to(n, k):
    return -(-n // k) * k


def gelu_parts(pre):
    pre = pre.astype(bf16)
    c0, c01, c03 = bf16(C0), bf16(C0 * C1), bf16(3 * C0 * C1)
    half, one = bf16(0.5), bf16(1.0)
    square = pre * pre
    t = jnp.tanh(pre * (c0 + c01 * square))
    hx = half * pre
    return hx + hx * t, (half + half * t) + hx * (one - t * t) * (c0 + c03 * square)


def bits_of(n):
    return n.bit_length() - 1


def reduce_unit(n_dp):
    return 16 * n_dp


def reduce_parts(half, unit, most=4):
    units = half // unit
    count = min(most, units)
    ends = [units * (k + 1) // count for k in range(count)]
    starts = [0] + ends[:-1]
    return [(a * unit, (b - a) * unit) for a, b in zip(starts, ends)]


def chain_kernel(n_dp, n_sec, live_ref, img_h, og_h, ac, sh, ls, pw_in, pb_in, wu_h, bu, wd_h, bd, out_h, gin_h, full,
                 img, og, xch, pw, rs, kk, aa, bdl, wus, wds, bus, stage, xw, xt, gw, gt, hid, slope, dpre,
                 gx, gd, gp, gsum, sd, bup, gdn, grad_o, work, recv,
                 in_sem, out_sem, w_sem, pair_send, pair_recv, send_sem, recv_sem, z_send, z_recv, g_send, g_recv):
    M, P, B, D = out_h.shape
    L, _, H = wus.shape
    PP = pw.shape[1]
    R = B * PP
    RC = R // 2 if R % 32 == 0 else R
    HC = H // 2 if H % 512 == 0 else H
    me, sec = lax.axis_index("dp"), lax.axis_index("section")
    own, odd = sec // 2, sec % 2
    low = sec < 2
    partner = (me, sec + 1 - 2 * odd)
    half_m = M // 2
    nb = bits_of(n_dp)
    half = full.shape[1] // 2
    parts = reduce_parts(half, reduce_unit(n_dp))
    n_part = len(parts)
    every = range(n_part)
    rest = list(range(1, nb))
    orders = [rest if k % 2 == 0 else rest[::-1] for k in every]
    bit = [(me // (1 << j)) % 2 for j in range(nb)]
    zbit = odd
    base = bit[0] * half

    def peer(j):
        return (me + (1 << j) - 2 * (1 << j) * bit[j], sec)

    def signal(device):
        pl.semaphore_signal(barrier, inc=1, device_id=device, device_id_type=pl.DeviceIdType.MESH)

    def copy(src, dst, s, r, device):
        return pltpu.make_async_remote_copy(src_ref=src, dst_ref=dst, send_sem=s, recv_sem=r, device_id=device, device_id_type=pl.DeviceIdType.MESH)

    def rows(b):
        return slice(b * PP, (b + 1) * PP)

    def span(off, n):
        return pl.ds(pl.multiple_of(off, 128 if n % 128 == 0 and n == HC else 16), n)

    def cols(b):
        return slice(b * D, (b + 1) * D)

    def vec(ref, k):
        return ref[k:k + 1, :].astype(f32)

    def micro(t):
        return lax.rem(t + half_m * odd, M)

    def needs(t, which):
        return (t < half_m) | ((sec == 3) if which else (sec < 3))

    def load(t, which):
        m = micro(t)
        return pltpu.make_async_copy((img_h, og_h)[which].at[m], (img, og)[which].at[m], in_sem.at[which, m])

    def save(which, m):
        return pltpu.make_async_copy((img, og)[which].at[m], (out_h, gin_h)[which].at[m], out_sem.at[which, m])

    def pair(src, dst, t):
        return copy(src, dst, pair_send.at[t], pair_recv.at[t], partner)

    barrier = pltpu.get_barrier_semaphore()
    for j in range(nb):
        signal(peer(j))

    @pl.when(sec > 0)
    def _():
        signal((me, sec - 1))

    @pl.when(sec < n_sec - 1)
    def _():
        signal((me, sec + 1))

    load(0, 0).start()
    w_up = pltpu.make_async_copy(wu_h, wus, w_sem.at[0])
    w_down = pltpu.make_async_copy(wd_h, wds, w_sem.at[1])
    w_up.start()
    w_down.start()
    load(0, 1).start()
    for t in range(1, M):
        for which in range(2):
            @pl.when(needs(t, which))
            def _():
                load(t, which).start()

    pw[...] = jnp.zeros_like(pw)
    pbt = jnp.concatenate([pb_in[...].astype(f32), jnp.zeros((8 - L, P), f32)], axis=0).T
    stage[...] = jnp.zeros_like(stage)
    for l in range(L):
        pw[l, :P, :P] = pw_in[:, l, :]
        rs[l] = jnp.sum(pw[l].astype(f32), axis=1, keepdims=True)
        stage[0:P, l:l + 1] = pbt[:, l:l + 1]
        kk[l] = vec(ls, 2 * l) * (vec(sh, 2 * l) * rs[l] + stage[0:PP, l:l + 1])
        aa[l] = vec(ac, 2 * l) * vec(ls, 2 * l)
        bdl[l] = vec(bd, l) * vec(ls, 2 * l + 1)
    stage[0:PP, 0:128] = jnp.zeros((PP, 128), f32)
    for r in (gx, gd, gp, gsum, sd, bup, gdn):
        r[...] = jnp.zeros_like(r)
    w_up.wait()
    w_down.wait()
    for l in range(L):
        acol = jnp.broadcast_to(vec(ac, 2 * l + 1), (8, D)).T[:, 0:1]
        shift8 = jnp.broadcast_to(vec(sh, 2 * l + 1), (8, D)).astype(bf16)
        for k in range(0, H, D):
            bus[l, :, k:k + D] = dot(shift8, wus[l, :, k:k + D])[0:1, :] + bu[l:l + 1, k:k + D].astype(f32)
            wus[l, :, k:k + D] = (wus[l, :, k:k + D].astype(f32) * acol).astype(bf16)
            wds[l, k:k + D, :] = (wds[l, k:k + D, :].astype(f32) * vec(ls, 2 * l + 1)).astype(bf16)
    pl.semaphore_wait(barrier, nb + jnp.where(sec > 0, 1, 0) + jnp.where(sec < n_sec - 1, 1, 0))

    def take(ref, m):
        v = jnp.swapaxes(ref[m].astype(f32), 0, 1)
        for b in range(B):
            stage[b * PP:b * PP + P, :] = v[b] * live_ref[b, m].astype(f32)
            stage[b * PP + P:(b + 1) * PP, :] = jnp.zeros((PP - P, D), f32)

    def turned(pieces):
        return jnp.swapaxes(jnp.stack([p[0:P, :] for p in pieces], axis=0), 0, 1).astype(bf16)

    def from_tall(value):
        value = value.astype(f32)
        return turned([value[rows(b), :] for b in range(B)])

    def from_wide(value):
        return turned([value[:, cols(b)].astype(f32) for b in range(B)])

    def patch_forward(l):
        mix = dot(pw[l], xw[l])
        new = [xw[l, :, cols(b)].astype(f32) + (aa[l] * mix[:, cols(b)] + kk[l]) for b in range(B)]
        xt[l] = jnp.concatenate(new, axis=0).astype(bf16)

    def ffn_forward(l):
        x = xt[l]
        h, s = gelu_parts(dot(x, wus[l]) + bus[l])
        hid[l] = h
        slope[l] = s
        new = x.astype(f32) + (dot(h, wds[l]) + bdl[l])
        for b in range(B):
            xw[l + 1, :, cols(b)] = new[rows(b), :].astype(bf16)

    def ffn_up(l):
        h, s = gelu_parts(dot(xt[l], wus[l]) + bus[l])
        hid[l] = h
        slope[l] = s

    def ffn_back(l):
        def piece_back(i, carry):
            q = span(i * RC, RC)
            g = gt[l + 1, q, :]
            d = (dot(g, wds[l], 1, 1) * slope[l, q, :].astype(f32)).astype(bf16)
            dpre[q, :] = d
            stage[q, :] = g.astype(f32) + dot(d, wus[l], 1, 1)
            return carry

        lax.fori_loop(0, R // RC, piece_back, 0)
        for b in range(B):
            gw[:, cols(b)] = stage[rows(b), :].astype(bf16)

    def back(l):
        ffn_back(l)
        moved = dot(pw[l], gw[...], 0, 0)
        new = [gw[:, cols(b)].astype(f32) + aa[l] * moved[:, cols(b)] for b in range(B)]
        gt[l] = jnp.concatenate(new, axis=0).astype(bf16)

        @pl.when(own == l)
        def _():
            gdn[...] += jnp.sum(gt[l + 1].astype(f32), axis=0, keepdims=True)
            x_t, g_t = xt[l].T, gt[l + 1].T

            def weight_piece(i, carry):
                q = span(i * HC, HC)
                gx[:, q] += dot(x_t, dpre[:, q])
                gd[:, q] += dot(g_t, hid[l, :, q])
                bup[:, q] += jnp.sum(dpre[:, q].astype(f32), axis=0, keepdims=True)
                return carry

            lax.fori_loop(0, H // HC, weight_piece, 0)
            scaled = jnp.concatenate([(gw[:, cols(b)].astype(f32) * aa[l]).astype(bf16) for b in range(B)], axis=1)
            gp[...] += dot(scaled, xw[l], 1, 1)
            mix = dot(pw[l], xw[l])
            for b in range(B):
                gb = gw[:, cols(b)].astype(f32)
                gsum[...] += gb
                sd[...] += jnp.sum(gb * mix[:, cols(b)], axis=0, keepdims=True)

    def read_images(t, m):
        load(t, 0).wait()
        take(img, m)
        for b in range(B):
            xw[0, :, cols(b)] = stage[rows(b), :].astype(bf16)

    def whole(t, carry):
        m = micro(t)
        other = lax.rem(m + half_m, M)
        read_images(t, m)
        patch_forward(0)
        ffn_forward(0)

        @pl.when(sec == 0)
        def _():
            img[m] = from_tall(xt[0])

        @pl.when(sec == 1)
        def _():
            img[m] = from_wide(xw[1])

        patch_forward(1)

        @pl.when(sec == 2)
        def _():
            img[m] = from_tall(xt[1])
            xch[t] = xt[1]
            pair(xch.at[t], xch.at[t], t).start()

        ffn_up(1)

        @pl.when(sec == 3)
        def _():
            new = xt[1].astype(f32) + (dot(hid[1], wds[1]) + bdl[1])
            img[m] = turned([new[rows(b), :] for b in range(B)])

        save(0, m).start()
        load(t, 1).wait()
        take(og, m)
        gt[L] = stage[...].astype(bf16)

        def half_back(i, carry):
            l = L - 1 - i
            back(l)

            @pl.when(sec == 3)
            def _():
                og[m] = from_wide(gw[...])
                og[M + t] = from_tall(gt[l])
                pair(og.at[M + t], gin_h.at[m], t).start()

            @pl.when(sec == 2)
            def _():
                og[m] = from_tall(gt[l])

            @pl.when(low & (l == 0))
            def _():
                og[jnp.where(odd == 0, other, m)] = from_wide(gw[...])
                og[jnp.where(odd == 0, m, other)] = from_tall(gt[l])
                pair(og.at[other], gin_h.at[m], t).start()
            return carry

        lax.fori_loop(0, jnp.where(low, L, 1), half_back, 0)
        save(1, m).start()
        return carry

    lax.fori_loop(0, half_m, whole, 0)

    for l in range(L):
        @pl.when(own == l)
        def _():
            acol = jnp.broadcast_to(vec(ac, 2 * l + 1), (8, D)).T[:, 0:1]
            ccol = jnp.broadcast_to(vec(sh, 2 * l + 1), (8, D)).T[:, 0:1]
            scale1 = jnp.zeros((D, 1), f32)
            shift1 = jnp.zeros((D, 1), f32)
            for k in range(0, H, D):
                g = gx[:, k:k + D]
                w = wus[l, :, k:k + D].astype(f32)
                b = bup[:, k:k + D]
                grad_o[k:k + D, :] = (acol * g + ccol * b).astype(bf16)
                scale1 += jnp.sum(w * g, axis=1, keepdims=True)
                shift1 += jnp.sum(w * b, axis=1, keepdims=True)
            gain1 = jnp.zeros((1, D), f32)
            for k in range(0, H, D):
                g = gd[:, k:k + D].T
                gain1 += jnp.sum(g * wds[l, k:k + D, :].astype(f32), axis=0, keepdims=True)
                grad_o[H + k:H + k + D, :] = (g * vec(ls, 2 * l + 1)).astype(bf16)
            gain1 = gain1 / vec(ls, 2 * l + 1) + vec(bd, l) * gdn[...]
            scale1, shift1 = scale1 / acol, shift1 / acol
            both = jnp.broadcast_to(jnp.concatenate([scale1, shift1], axis=1), (D, 2)).T
            gs = gsum[...]
            lsrow, crow = vec(ls, 2 * l), vec(sh, 2 * l)
            wsum = jnp.sum(gs * rs[l], axis=0, keepdims=True)
            stage[0:PP, 0:PP] = gp[...] + jnp.sum(gs * (lsrow * crow), axis=1, keepdims=True)
            stage[0:PP, 256:257] = jnp.zeros((PP, 1), f32)
            stage[0:P, 256:257] = pbt[:, l:l + 1]
            psum = jnp.sum(gs * stage[0:PP, 256:257], axis=0, keepdims=True)
            offset = jnp.broadcast_to(jnp.sum(gs * lsrow, axis=1, keepdims=True), (PP, 8)).T[0:1, :]
            s_row = sd[...]
            extra = P + SMALL_ROWS

            def put(k, row):
                stage[P + k:P + k + 1, 0:row.shape[1]] = row
            stage[P:extra, :] = jnp.zeros((SMALL_ROWS, D), f32)
            put(ROW_SCALE, lsrow * s_row)
            put(ROW_SCALE + 1, both[0:1, :])
            put(ROW_SHIFT, lsrow * wsum)
            put(ROW_SHIFT + 1, both[1:2, :])
            put(ROW_GAIN, vec(ac, 2 * l) * s_row + crow * wsum + psum)
            put(ROW_GAIN + 1, gain1)
            put(ROW_OFFSET, offset[:, 0:P])
            for k in range(H // D):
                put(ROW_UPB + k, bup[:, k * D:(k + 1) * D])
            put(ROW_UPB + H // D, vec(ls, 2 * l + 1) * gdn[...])
            grad_o[2 * H:2 * H + extra, :] = stage[0:extra, :].astype(bf16)
    grad_o[2 * H + P + SMALL_ROWS:, :] = jnp.zeros((grad_o.shape[0] - 2 * H - P - SMALL_ROWS, D), bf16)

    def at_step(k, t):
        off, n = jnp.int32(parts[k][0]), parts[k][1]
        for j in orders[k][:t - 1]:
            n = n // 2
            off = off + bit[j] * n
        if t > nb:
            n = n // 2
            off = off + zbit * n
        return off, n

    def exchange(k, t):
        if t == 0:
            off, n = parts[k]
            return copy(grad_o.at[span((1 - bit[0]) * half + off, n)], recv.at[pl.ds(2 * off, n)], send_sem.at[k, 0], recv_sem.at[k, 0], peer(0)), 2 * off
        off, n = at_step(k, t)
        b, device = (bit[orders[k][t - 1]], peer(orders[k][t - 1])) if t < nb else (zbit, partner)
        slot = 2 * parts[k][0] + sum(parts[k][1] >> u for u in range(t))
        return copy(work.at[span(off + (1 - b) * (n // 2), n // 2)], recv.at[pl.ds(slot, n // 2)], send_sem.at[k, t], recv_sem.at[k, t], device), slot

    def add_step(t):
        for k in every:
            c, slot = exchange(k, t)
            c.wait_recv()
            off, n = at_step(k, t + 1)
            piece_rows = parts[k][1] >> nb

            def add(i, carry):
                at = i * piece_rows
                mine = grad_o[span(base + off + at, piece_rows), :] if t == 0 else work[span(off + at, piece_rows), :]
                total = (mine.astype(f32) + recv[span(slot + at, piece_rows), :].astype(f32)).astype(bf16)
                if t < nb:
                    work[span(off + at, piece_rows), :] = total
                else:
                    full[own, span(base + off + at, piece_rows), :] = total
                return carry

            lax.fori_loop(0, n // piece_rows, add, 0)
            if t < nb:
                exchange(k, t + 1)[0].start()
            else:
                for d in range(2):
                    z_send_item(0, d, k)

    place, size = zip(*[at_step(k, nb + 1) for k in every])

    def piece(k, j):
        return full.at[j // 2, span(base + place[k] + (j % 2 - zbit) * size[k], size[k])]

    def z_case(dist, d):
        j, target = (sec - dist, sec + 1) if d == 0 else (sec + dist, sec - 1)
        return j, target, ((j >= 0) & (target < n_sec)) if d == 0 else ((j < n_sec) & (target >= 0))

    def z_copy(dist, d, k, j, target):
        return copy(piece(k, j), piece(k, j), z_send.at[k, d, dist], z_recv.at[k, d, dist], (me, target))

    def z_send_item(dist, d, k):
        j, target, ok = z_case(dist, d)

        @pl.when(ok)
        def _():
            z_copy(dist, d, k, j, target).start()

    def z_wait_send(dist, d, k):
        j, target, ok = z_case(dist, d)

        @pl.when(ok)
        def _():
            z_copy(dist, d, k, j, target).wait_send()

    def z_wait_recv(dist, d, k):
        j = sec - dist - 1 if d == 0 else sec + dist + 1

        @pl.when((j >= 0) & (j < n_sec))
        def _():
            z_copy(dist, d, k, j, sec).wait_recv()

    def region(k, t):
        order = orders[k]
        off, n = jnp.int32(parts[k][0]), parts[k][1]
        for j in order[:len(order) - t]:
            n = n // 2
            off = off + bit[j] * n
        return off, n

    def g_copy(w, k, t, l):
        off, n = region(k, t)
        ref = full.at[l, span(base + off, n)]
        return copy(ref, ref, g_send.at[w, k, t], g_recv.at[w, k, t], peer(orders[k][len(orders[k]) - 1 - t]))

    def c_copy(w, k, l):
        ref = full.at[l, span(base + parts[k][0], parts[k][1])]
        return copy(ref, ref, g_send.at[w, k, nb - 1], g_recv.at[w, k, nb - 1], peer(0))

    layers = [own] + [(own + i) % L for i in range(1, L)]
    steps = nb - 1

    def gather(w, t):
        for k in every:
            g_copy(w, k, t, layers[w]).wait_recv()
            if t + 1 < steps:
                g_copy(w, k, t + 1, layers[w]).start()
            else:
                c_copy(w, k, layers[w]).start()

    def line(dist):
        for k in every:
            for d in range(2):
                z_wait_recv(dist, d, k)
            if dist < n_sec - 2:
                for d in range(2):
                    z_send_item(dist + 1, d, k)
            if dist == 0:
                g_copy(0, k, 0, layers[0]).start()
            if dist == n_sec - 2:
                for w in range(1, L):
                    g_copy(w, k, 0, layers[w]).start()

    waves = [functools.partial(add_step, t) for t in range(nb + 1)]
    waves.append(functools.partial(line, 0))
    for dist in range(1, n_sec - 1):
        waves.append(functools.partial(line, dist))
        if dist <= steps:
            waves.append(functools.partial(gather, 0, dist - 1))
    for t in range(min(n_sec - 2, steps), steps):
        waves.append(functools.partial(gather, 0, t))
    for w in range(1, L):
        for t in range(steps):
            waves.append(functools.partial(gather, w, t))

    def rest_forward(t):
        m = micro(t)

        @pl.when(sec < 3)
        def _():
            read_images(t, m)
            patch_forward(0)

        @pl.when(sec == 0)
        def _():
            img[m] = from_tall(xt[0])

        @pl.when(sec == 3)
        def _():
            slot = t - half_m
            pair(xch.at[slot], xch.at[slot], slot).wait_recv()
            xt[1] = xch[slot]

        @pl.when(sec > 0)
        def _():
            l = jnp.where(sec == 3, 1, 0)
            ffn_forward(l)

            @pl.when(sec != 2)
            def _():
                img[m] = from_wide(xw[l + 1])

        @pl.when(sec == 2)
        def _():
            patch_forward(1)
            img[m] = from_tall(xt[1])

        save(0, m).start()

    def rest_backward(t):
        m = micro(t)

        @pl.when(sec == 3)
        def _():
            load(t, 1).wait()
            take(og, m)
            gt[L] = stage[...].astype(bf16)
            ffn_back(L - 1)
            og[m] = from_wide(gw[...])
            save(1, m).start()

    for k in every:
        exchange(k, 0)[0].start()
    beside = 2 * (M - half_m)

    def rest_step(t, carry):
        for i, piece_of_work in enumerate((rest_forward, rest_backward)):
            piece_of_work(t)
            for n in range(i, min(beside, len(waves)), 2):
                @pl.when(t == half_m + n // 2)
                def _():
                    waves[n]()
        return carry

    lax.fori_loop(half_m, M, rest_step, 0)
    for wave in waves[beside:]:
        wave()
    for w in range(L):
        for k in every:
            c_copy(w, k, layers[w]).wait_recv()

    for k in every:
        for t in range(nb + 1):
            exchange(k, t)[0].wait_send()
        for w in range(L):
            for t in range(steps):
                g_copy(w, k, t, layers[w]).wait_send()
            c_copy(w, k, layers[w]).wait_send()
        for dist in range(n_sec - 1):
            for d in range(2):
                z_wait_send(dist, d, k)
    for t in range(M):
        m = micro(t)
        save(0, m).wait()

        @pl.when((t < half_m) | (sec == 3))
        def _():
            save(1, m).wait()
    for t in range(half_m):
        @pl.when(sec == 2)
        def _():
            pair(xch.at[t], xch.at[t], t).wait_send()

        @pl.when(sec != 2)
        def _():
            pair(og.at[t], gin_h.at[t], t).wait_send()

        @pl.when(sec != 3)
        def _():
            pair(og.at[t], gin_h.at[t], t).wait_recv()


def chain_call(n_dp, n_sec, images, out_grad, live, ac, sh, ls, pw, pb, wu, bu, wd, bd):
    M, P, B, D = images.shape
    L, _, H = wu.shape
    PP = up_to(P, 8)
    R = B * PP
    total = up_to(2 * H + P + SMALL_ROWS, 2 * reduce_unit(n_dp))
    nb = bits_of(n_dp)
    n_part = len(reduce_parts(total // 2, reduce_unit(n_dp)))
    vm = pl.BlockSpec(memory_space=pltpu.VMEM)
    hbm = pl.BlockSpec(memory_space=pl.ANY)
    sem = pltpu.SemaphoreType.DMA
    return pl.pallas_call(
        functools.partial(chain_kernel, n_dp, n_sec),
        in_specs=[pl.BlockSpec(memory_space=pltpu.SMEM), hbm, hbm, vm, vm, vm, vm, vm, hbm, vm, hbm, vm],
        out_specs=[hbm, hbm, vm],
        out_shape=[jax.ShapeDtypeStruct(images.shape, bf16)] * 2 + [jax.ShapeDtypeStruct((L, total, D), bf16)],
        scratch_shapes=[
            pltpu.VMEM((M, P, B, D), bf16), pltpu.VMEM((M + M // 2, P, B, D), bf16), pltpu.VMEM((M // 2, R, D), bf16),
            pltpu.VMEM((L, PP, PP), bf16), pltpu.VMEM((L, PP, 1), f32), pltpu.VMEM((L, PP, D), f32), pltpu.VMEM((L, 1, D), f32), pltpu.VMEM((L, 1, D), f32),
            pltpu.VMEM((L, D, H), bf16), pltpu.VMEM((L, H, D), bf16), pltpu.VMEM((L, 1, H), f32),
            pltpu.VMEM((R, D), f32),
            pltpu.VMEM((L + 1, PP, B * D), bf16), pltpu.VMEM((L, R, D), bf16), pltpu.VMEM((PP, B * D), bf16), pltpu.VMEM((L + 1, R, D), bf16),
            pltpu.VMEM((L, R, H), bf16), pltpu.VMEM((L, R, H), bf16), pltpu.VMEM((R, H), bf16),
            pltpu.VMEM((D, H), f32), pltpu.VMEM((D, H), f32), pltpu.VMEM((PP, PP), f32), pltpu.VMEM((PP, D), f32),
            pltpu.VMEM((1, D), f32), pltpu.VMEM((1, H), f32), pltpu.VMEM((1, D), f32),
            pltpu.VMEM((total, D), bf16), pltpu.VMEM((total // 2, D), bf16), pltpu.VMEM((total, D), bf16),
            sem((2, M)), sem((2, M)), sem((2,)), sem((M // 2,)), sem((M // 2,)),
            sem((n_part, nb + 1)), sem((n_part, nb + 1)), sem((n_part, 2, n_sec)), sem((n_part, 2, n_sec)),
            sem((L, n_part, nb)), sem((L, n_part, nb)),
        ],
        compiler_params=pltpu.CompilerParams(collective_id=1, has_side_effects=True, vmem_limit_bytes=62 * 2**20),
        name="chain",
    )(live, images, out_grad, ac, sh, ls, pw, pb, wu, bu, wd, bd)


def finish_kernel(P, up_rows, down_rows, tail_rows, x_i, g_i, scale_o, shift_o, gain_o, pw_o, off_o, up_o, upb_o, down_o, dnb_o, x_o, g_o):
    L = pw_o.shape[1]
    D, width = up_o.shape[1:]
    step = pl.program_id(0)
    x_o[...] = x_i[...]
    g_o[...] = g_i[...]
    for k in range(0, width, D):
        up_o[0, :, k:k + D] = up_rows[0, k:k + D, :].astype(f32)
    down_o[...] = down_rows[...].astype(f32)
    for l in range(L):
        @pl.when((step == l) & (pl.program_id(1) == 0))
        def _():
            tail = tail_rows[0, 0:up_to(P + SMALL_ROWS, 16), :].astype(f32)
            small = tail[P:P + SMALL_ROWS, :]
            pw_o[:, l, :] = tail[0:P, 0:P]
            for out, row in ((scale_o, ROW_SCALE), (shift_o, ROW_SHIFT), (gain_o, ROW_GAIN)):
                out[2 * l:2 * l + 2, :] = small[row:row + 2, :]
            off_o[l:l + 1, :] = small[ROW_OFFSET:ROW_OFFSET + 1, 0:P]
            last = upb_o.shape[1] // D
            for k in range(last):
                upb_o[l:l + 1, k * D:(k + 1) * D] = small[ROW_UPB + k:ROW_UPB + k + 1, :]
            dnb_o[l:l + 1, :] = small[ROW_UPB + last:ROW_UPB + last + 1, :]


def finish_call(full, outputs, in_grads, H):
    L, _, D = full.shape
    M, P, B, _ = outputs.shape
    steps = 1
    shape = (M, P, B, D)
    n = M // (L * steps)
    const = lambda *dims: pl.BlockSpec(dims, lambda i, c: (0,) * len(dims))
    acts = lambda: pl.BlockSpec((n,) + shape[1:], lambda i, c: (i * steps + c, 0, 0, 0))
    up_spec = pl.BlockSpec((1, D, H // steps), lambda i, c: (i, 0, c))
    down_spec = pl.BlockSpec((1, H // steps, D), lambda i, c: (i, c, 0))
    tail = up_to(P + SMALL_ROWS, 256)
    outs = pl.pallas_call(
        functools.partial(finish_kernel, P),
        grid=(L, steps),
        in_specs=[pl.BlockSpec((1, H // steps, D), lambda i, c: (i, c, 0)), pl.BlockSpec((1, H // steps, D), lambda i, c: (i, steps + c, 0)),
                  pl.BlockSpec((1, tail, D), lambda i, c: (i, 2 * H // tail, 0)), acts(), acts()],
        out_specs=[const(2 * L, D), const(2 * L, D), const(2 * L, D), const(P, L, P), const(L, P), up_spec, const(L, H), down_spec, const(L, D), acts(), acts()],
        out_shape=[jax.ShapeDtypeStruct(s, f32) for s in ((2 * L, D), (2 * L, D), (2 * L, D), (P, L, P), (L, P), (L, D, H), (L, H), (L, H, D), (L, D))]
        + [jax.ShapeDtypeStruct(shape, bf16)] * 2,
        compiler_params=pltpu.CompilerParams(vmem_limit_bytes=62 * 2**20),
        name="finish",
    )(full, full, full, outputs.reshape(shape), in_grads.reshape(shape))
    return tuple(outs[:9]) + tuple(a.reshape(M, P, B, D) for a in outs[9:])


def shards(n_dp, n_sec, images, out_grad, padding, affine_scale, affine_shift, layer_scale, patch_weight, patch_bias, up_weight, up_bias, down_weight, down_bias):
    outputs, in_grads, full = chain_call(
        n_dp, n_sec,
        images.transpose(0, 2, 1, 3), out_grad.transpose(0, 2, 1, 3), padding.T,
        affine_scale, affine_shift, layer_scale, patch_weight.transpose(1, 0, 2), patch_bias,
        up_weight, up_bias, down_weight, down_bias,
    )
    scale, shift, gain, slopes, offset, up, upb, down, dnb, outputs, in_grads = finish_call(full, outputs, in_grads, up_weight.shape[2])
    native = lambda a: a.transpose(0, 2, 1, 3)[None]
    return native(outputs), native(in_grads), scale, shift, gain, slopes.transpose(1, 0, 2), offset, up, upb, down, dnb


def solution(mesh):
    split = P(None, "dp", None, None)
    return jax.shard_map(
        functools.partial(shards, mesh.shape["dp"], mesh.shape["section"]),
        mesh=mesh,
        in_specs=(split, split, P(None, "dp")) + (P(),) * 9,
        out_specs=(P("section", None, "dp", None, None),) * 2 + (P(),) * 9,
        check_vma=False,
    )
```
